128 devices in a mesh: tm: 4 (over y), rest: 32 (over x, z, core).
Axes of the slice: x: 4, y: 4, z: 4, core: 2. Of those that a mesh axis runs over, the one named last changes fastest.
Arguments:
- slab: float32 [1024, 131072], P('tm', 'rest')
- start_basis: float32 [1024, 128], replicated, may hold values from -6 to 6
- time_rank: int32 [1], replicated, may hold values from 64 to 128
Outputs:
- basis: float32 [1024, 128], replicated
- core: float32 [128, 131072], P('tm', 'rest')
- param_gram: float32 [128, 128], replicated
The draws below stay inside these ranges and needn't reach their ends.
All inputs are finite; a program needn't handle non-finite values.
Results may differ from the reference program's by a relative error of at most 0.0003.
Values sent between devices are 32-bit elements; how exact they have to be, the bound alone decides.
No kernel may reach another device: no remote copies, remote signals or barrier semaphores. Data moves between devices by JAX's collectives and lax.ppermute only.
A program may use at most 128 MiB of HBM per device.

```python
import jax
import jax.numpy as jnp
from jax import lax

TIME = 1024
RANK = 128
PARAMS = 128
ITERS = 3
SPACE = 1024
COLUMNS = 131072


def draw_slab(key, part):
    key = jax.random.fold_in(key, 11)
    k_row, k_col, k_val = jax.random.split(key, 3)
    row_scale = jnp.exp(jax.random.uniform(k_row, (TIME, 1), jnp.float32, jnp.log(0.3), jnp.log(3.0)))
    place = jnp.arange(COLUMNS, dtype=jnp.float32)[None, :] / float(COLUMNS)
    col_scale = jnp.exp(jnp.log(3.0) * place) * jnp.exp(jax.random.uniform(k_col, (1, COLUMNS), jnp.float32, jnp.log(0.5), jnp.log(2.0)))
    values = jax.random.normal(k_val, (TIME, COLUMNS), jnp.float32)
    return jnp.clip(values * row_scale * col_scale, -40.0, 40.0)


def gaussian(rng, shape, scale, most, kind=jnp.bfloat16):
    entries = jax.random.normal(rng, shape, jnp.float32) * scale
    return jnp.minimum(jnp.maximum(entries, -most), most).astype(kind)


def setup_inputs(seed: int = 0) -> dict:
    keys = jax.random.split(jax.random.key(seed), 4)
    return {
        "slab": draw_slab(jax.random.fold_in(keys[3], 71), 0),
        "start_basis": gaussian(keys[1], (TIME, RANK), 1.0, 6.0, jnp.float32),
        "time_rank": jax.random.randint(keys[2], (1,), RANK // 2, RANK + 1).astype(jnp.int32),
    }


def reference(slab, start_basis, time_rank):
    hi = lax.Precision.HIGHEST
    gram = jnp.dot(slab.astype(jnp.float32), slab.T.astype(jnp.float32), precision=hi, preferred_element_type=jnp.float32) / float(COLUMNS)
    basis_iter = start_basis
    for step in range(ITERS):
        image = jnp.dot(gram.astype(jnp.float32), basis_iter.astype(jnp.float32), precision=hi, preferred_element_type=jnp.float32)
        inner = jnp.dot(image.T.astype(jnp.float32), image.astype(jnp.float32), precision=hi, preferred_element_type=jnp.float32)
        lower = jnp.linalg.cholesky(inner)
        basis_iter = lax.linalg.triangular_solve(lower, image.T, left_side=True, lower=True).T
    keep = (jnp.arange(RANK, dtype=jnp.int32) < time_rank[0]).astype(jnp.float32)
    basis = basis_iter * keep[None, :]
    core = jnp.dot(basis.T.astype(jnp.float32), slab.astype(jnp.float32), precision=hi, preferred_element_type=jnp.float32)
    folded = core.reshape(RANK * SPACE, PARAMS)
    param_gram = jnp.dot(folded.T.astype(jnp.float32), folded.astype(jnp.float32), precision=hi, preferred_element_type=jnp.float32) / float(RANK * SPACE)
    return (basis, core, param_gram)
```

```python
import jax
import jax.numpy as jnp
from jax import lax
from jax.experimental import pallas as pl
from jax.experimental.pallas import tpu as pltpu
from jax.sharding import PartitionSpec as P

PARAMS = 128
ITERS = 3
NY, NX, NZ = 4, 4, 4
PAIRS = [(i, j) for i in range(NY) for j in range(i, NY)]


def rest_index(x, z, c):
    return (x * NZ + z) * 2 + c


def along_y(v, k):
    return lax.ppermute(v, "tm", [(i, (i + k) % NY) for i in range(NY)])


def along_core(v):
    return lax.ppermute(v, "rest", [(i, i ^ 1) for i in range(2 * NX * NZ)])


def along_xz(v, k, first):
    perm = []
    for x in range(NX):
        for z in range(NZ):
            for c in range(2):
                if (c == 0) == first:
                    to = rest_index((x + k) % NX, z, c)
                else:
                    to = rest_index(x, (z + k) % NZ, c)
                perm.append((rest_index(x, z, c), to))
    return lax.ppermute(v, "rest", perm)


def split_bf16(v):
    hi = v.astype(jnp.bfloat16)
    lo = (v - hi.astype(jnp.float32)).astype(jnp.bfloat16)
    return hi, lo


def dot_t(a, b):
    return lax.dot_general(a, b, (((1,), (1,)), ((), ())), preferred_element_type=jnp.float32)


def gram_kernel(place_ref, w0, w1, w2, w3, out_ref, hi_ref, lo_ref):
    for k, w in enumerate((w0, w1, w2, w3)):
        hi, lo = split_bf16(w[...])
        hi_ref[place_ref[k]] = hi
        lo_ref[place_ref[k]] = lo
    for n, (i, j) in enumerate(PAIRS):
        out_ref[n] = dot_t(hi_ref[i], hi_ref[j]) + (dot_t(hi_ref[i], lo_ref[j]) + dot_t(lo_ref[i], hi_ref[j]))


def partial_gram(place, parts):
    rows, cols = parts[0].shape
    return pl.pallas_call(
        gram_kernel,
        out_shape=jax.ShapeDtypeStruct((len(PAIRS), rows, rows), jnp.float32),
        in_specs=[pl.BlockSpec(memory_space=pltpu.SMEM)] + [pl.BlockSpec(memory_space=pltpu.VMEM)] * 4,
        out_specs=pl.BlockSpec(memory_space=pltpu.VMEM),
        scratch_shapes=[pltpu.VMEM((NY, rows, cols), jnp.bfloat16)] * 2,
        compiler_params=pltpu.CompilerParams(vmem_limit_bytes=40 * 2**20),
        cost_estimate=pl.CostEstimate(flops=2 * 30 * rows * rows * cols, bytes_accessed=7 * 2**20, transcendentals=0),
    )(place, *parts)


def take(v, i):
    return lax.dynamic_index_in_dim(v, i, 0, keepdims=False)


def ordered(pieces, me):
    out = jnp.zeros((NY,) + pieces[0].shape, pieces[0].dtype)
    for k, piece in enumerate(pieces):
        out = lax.dynamic_update_index_in_dim(out, piece, (me - k) % NY, 0)
    return out


def scatter_sum(v, me, move):
    got = [move(take(v, (me + k) % NY), k) for k in (1, 3, 2)]
    return take(v, me) + got[0] + got[1] + got[2]


def exchange_sum(v, move):
    got = [move(v, k) for k in (1, 3, 2)]
    return v + got[0] + got[1] + got[2]


def gather(v, me, move):
    got = {k: move(v, k) for k in (1, 3, 2)}
    return ordered([v, got[1], got[2], got[3]], me)


def all_sum(v, core, first_me, second_me):
    shape = v.shape
    size = v.size // 32
    v = v.reshape(2, NX, NZ, size // 128, 128)
    v = take(v, core) + along_core(take(v, 1 - core))
    v = scatter_sum(v, first_me, lambda u, k: along_xz(u, k, True))
    v = scatter_sum(v, second_me, lambda u, k: along_xz(u, k, False))
    v = exchange_sum(v, along_y)
    v = gather(v, second_me, lambda u, k: along_xz(u, k, False))
    v = gather(v, first_me, lambda u, k: along_xz(u, k, True))
    other = along_core(v)
    out = jnp.where(core == 0, jnp.stack([v, other]), jnp.stack([other, v]))
    return out.reshape(shape)


def local(slab, start_basis, time_rank):
    hi = lax.Precision.HIGHEST
    rest_count = lax.axis_size("rest")
    time_local, columns_local = slab.shape
    columns_all = columns_local * rest_count
    width = columns_local // NY
    me_y = lax.axis_index("tm")
    rest = lax.axis_index("rest")
    core_id, me_z, me_x = rest % 2, (rest // 2) % NZ, rest // (2 * NZ)
    first_me = jnp.where(core_id == 0, me_x, me_z)
    second_me = jnp.where(core_id == 0, me_z, me_x)

    def columns(k):
        return lax.dynamic_slice_in_dim(slab, (me_y + k) % NY * width, width, 1)

    got = {k: along_y(columns(k), k) for k in (1, 3, 2)}
    parts = [columns(0), got[1], got[2], got[3]]
    place = (me_y - jnp.arange(NY, dtype=jnp.int32)) % NY
    packed = all_sum(partial_gram(place, parts), core_id, first_me, second_me) / float(columns_all)
    index = {pair: n for n, pair in enumerate(PAIRS)}
    gram = jnp.concatenate(
        [
            jnp.concatenate([packed[index[i, j]] if i <= j else packed[index[j, i]].T for j in range(NY)], 1)
            for i in range(NY)
        ],
        0,
    )
    basis_iter = start_basis
    for step in range(ITERS):
        image = jnp.dot(gram, basis_iter, precision=hi, preferred_element_type=jnp.float32)
        inner = jnp.dot(image.T, image, precision=hi, preferred_element_type=jnp.float32)
        lower = jnp.linalg.cholesky(inner)
        basis_iter = lax.linalg.triangular_solve(lower, image.T, left_side=True, lower=True).T
    rank_all = basis_iter.shape[1]
    keep = (jnp.arange(rank_all, dtype=jnp.int32) < time_rank[0]).astype(jnp.float32)
    basis = basis_iter * keep[None, :]

    core = sum(
        jnp.dot(
            lax.dynamic_slice_in_dim(basis, (me_y - k) % NY * time_local, time_local, 0).T,
            parts[k],
            precision=lax.Precision.HIGH,
            preferred_element_type=jnp.float32,
        )
        for k in range(NY)
    )
    folded = core.reshape(-1, PARAMS)
    param = jnp.dot(folded.T, folded, precision=lax.Precision.HIGH, preferred_element_type=jnp.float32)
    param = param + along_core(param)
    param = exchange_sum(param, lambda u, k: along_xz(u, k, True))
    param = exchange_sum(param, lambda u, k: along_xz(u, k, False))
    param = exchange_sum(param, along_y)
    space_all = columns_local // PARAMS * rest_count
    param_gram = param / float(rank_all * space_all)

    slots = core.reshape(NY, rank_all // NY, width)
    mine = {k: along_y(take(slots, (me_y + k) % NY), k) for k in (1, 3, 2)}
    mine[0] = take(slots, me_y)
    core_out = jnp.zeros((rank_all // NY, columns_local), jnp.float32)
    for k in range(NY):
        core_out = lax.dynamic_update_slice_in_dim(core_out, mine[k], (me_y - k) % NY * width, 1)
    return (basis, core_out, param_gram)


def solution(mesh):
    in_specs = (P("tm", "rest"), P(), P())
    out_specs = (P(), P("tm", "rest"), P())
    return jax.shard_map(local, mesh=mesh, in_specs=in_specs, out_specs=out_specs, check_vma=False)
```

```python
import jax
import jax.numpy as jnp
from jax import lax
from jax.experimental import pallas as pl
from jax.experimental.pallas import tpu as pltpu
from jax.sharding import PartitionSpec as P

F32, BF16 = jnp.float32, jnp.bfloat16
PARAMS = 128
ITERS = 3
NY, NX, NZ = 4, 4, 4
PAIRS = [(i, j) for i in range(NY) for j in range(i, NY)]
HALF = len(PAIRS) // 2
VMEM, SMEM = pltpu.VMEM, pltpu.SMEM


def rest_index(x, z, c):
    return (x * NZ + z) * 2 + c


def along_y(v, k):
    return lax.ppermute(v, "tm", [(i, (i + k) % NY) for i in range(NY)])


def along_core(v):
    return lax.ppermute(v, "rest", [(i, i ^ 1) for i in range(2 * NX * NZ)])


def along_xz(v, k, first):
    perm = []
    for x in range(NX):
        for z in range(NZ):
            for c in range(2):
                if (c == 0) == first:
                    to = rest_index((x + k) % NX, z, c)
                else:
                    to = rest_index(x, (z + k) % NZ, c)
                perm.append((rest_index(x, z, c), to))
    return lax.ppermute(v, "rest", perm)


def split2(v):
    hi = v.astype(BF16)
    return hi, (v - hi.astype(F32)).astype(BF16)


def split3(v):
    hi = v.astype(BF16)
    rest = v - hi.astype(F32)
    mid = rest.astype(BF16)
    return hi, mid, (rest - mid.astype(F32)).astype(BF16)


def dot(a, b, ca, cb):
    return lax.dot_general(a, b, (((ca,), (cb,)), ((), ())), preferred_element_type=F32)


def gram_kernel(table, w0, w1, w2, w3, send, keep, hi_out, lo_out, hi, lo, sem):
    for k, w in enumerate((w0, w1, w2, w3)):
        h, l = split2(w[...])
        hi[table[k]] = h
        lo[table[k]] = l
    copies = [
        pltpu.make_async_copy(hi, hi_out, sem.at[0]),
        pltpu.make_async_copy(lo, lo_out, sem.at[1]),
    ]
    for copy in copies:
        copy.start()
    for n in range(2 * HALF):
        i, j = table[NY + 2 * n], table[NY + 2 * n + 1]
        out = send if n < HALF else keep
        out[n % HALF] = dot(hi[i], hi[j], 1, 1) + (
            (dot(hi[i], lo[j], 1, 1) + dot(lo[i], hi[j], 1, 1)) + dot(lo[i], lo[j], 1, 1)
        )
    for copy in copies:
        copy.wait()


def partial_gram(table, parts):
    rows, cols = parts[0].shape
    blocks = jax.ShapeDtypeStruct((HALF, rows, rows), F32)
    halves = jax.ShapeDtypeStruct((NY, rows, cols), BF16)
    return pl.pallas_call(
        gram_kernel,
        out_shape=(blocks, blocks, halves, halves),
        in_specs=[pl.BlockSpec(memory_space=SMEM)] + [pl.BlockSpec(memory_space=VMEM)] * 4,
        out_specs=[pl.BlockSpec(memory_space=VMEM)] * 2 + [pl.BlockSpec(memory_space=pl.ANY)] * 2,
        scratch_shapes=[VMEM((NY, rows, cols), BF16)] * 2 + [pltpu.SemaphoreType.DMA((2,))],
        compiler_params=pltpu.CompilerParams(vmem_limit_bytes=40 * 2**20),
        cost_estimate=pl.CostEstimate(flops=2 * 40 * rows * rows * cols, bytes_accessed=11 * 2**20, transcendentals=0),
        name="partial_gram",
    )(table, *parts)


def row_of(v, k):
    return jnp.broadcast_to(v[k : k + 1, :], v.shape)


def cholesky_inverse(work):
    n = work.shape[0]
    r = lax.broadcasted_iota(jnp.int32, (n, n), 0)
    c = lax.broadcasted_iota(jnp.int32, (n, n), 1)
    work[:, n:] = (r == c).astype(F32)
    row = lax.broadcasted_iota(jnp.int32, (8, n), 0)
    panels = []
    for p in range(n // 8):
        left, right = work[8 * p : 8 * p + 8, :n], work[8 * p : 8 * p + 8, n:]
        column = [jnp.broadcast_to(left[:, 8 * p + j : 8 * p + j + 1], (8, n)) for j in range(8)]
        scale = jnp.zeros((8, n), F32)
        for k in range(8):
            pivot = row_of(column[k], k)
            factor = jnp.where(row > k, column[k] * (1.0 / pivot), 0.0)
            scale = jnp.where(row == k, lax.rsqrt(pivot), scale)
            for j in range(k + 1, 8):
                column[j] = column[j] - factor * row_of(column[j], k)
            if k < 7:
                left = left - factor * row_of(left, k)
                right = right - factor * row_of(right, k)
        left, right = left * scale, right * scale
        panels.append(right)
        if p < n // 8 - 1:
            h, m, l = split3(jnp.concatenate([left, right], 1))
            lh, lm, ll = h[:, :n], m[:, :n], l[:, :n]
            work[...] = work[...] - dot(
                jnp.concatenate([lh, lh, lm, lm, lh, ll], 0), jnp.concatenate([h, m, h, m, l, h], 0), 0, 0
            )
    return jnp.concatenate(panels, 0)


def solve_kernel(
    place, rank, *refs, scale
):
    pieces, (start, hi_in, lo_in) = refs[:8], refs[8:11]
    basis_out, core0, core1, core2, core3, param_out = refs[11:17]
    packed, gh, gm, gl, hi, lo, work, core, sem = refs[17:]
    copies = [
        pltpu.make_async_copy(hi_in, hi, sem.at[0]),
        pltpu.make_async_copy(lo_in, lo, sem.at[1]),
    ]
    for copy in copies:
        copy.start()
    rows = pieces[0].shape[1]
    for n, piece in enumerate(pieces):
        for j in range(NX):
            at = pl.multiple_of(place[NY + NX * n + j] * rows, 8)
            packed[pl.ds(at, rows), :] = piece[j]
    t = packed.shape[1]
    for n, (i, j) in enumerate(PAIRS):
        block = packed[n * t : (n + 1) * t, :] * scale
        for k, g in enumerate(split3(block)):
            (gh, gm, gl)[k][i * t : (i + 1) * t, j * t : (j + 1) * t] = g
        if i < j:
            for k, g in enumerate(split3(block.T)):
                (gh, gm, gl)[k][j * t : (j + 1) * t, i * t : (i + 1) * t] = g

    q = start[...].T
    n = q.shape[0]
    for _ in range(ITERS):
        h, m, l = split3(q)
        by_h = dot(jnp.concatenate([h, m, l], 0), gh[...], 1, 0)
        by_m = dot(jnp.concatenate([h, m], 0), gm[...], 1, 0)
        by_l = dot(h, gl[...], 1, 0)
        image = by_h[:n] + ((by_h[n : 2 * n] + by_m[:n]) + (by_h[2 * n :] + by_m[n:] + by_l))
        h, m, l = split3(image)
        by_h = dot(jnp.concatenate([h, m, l], 0), h, 1, 1)
        small = by_h[n : 2 * n] + by_h[2 * n :]
        work[:, :n] = by_h[:n] + ((small + small.T) + dot(m, m, 1, 1))
        ih, im, il = split3(cholesky_inverse(work))
        by_h = dot(jnp.concatenate([ih, im, il], 0), h, 1, 0)
        by_m = dot(jnp.concatenate([ih, im], 0), m, 1, 0)
        q = by_h[:n] + ((by_h[n : 2 * n] + by_m[:n]) + (by_h[2 * n :] + by_m[n:] + dot(ih, l, 1, 0)))

    slot = lax.broadcasted_iota(jnp.int32, q.shape, 0)
    q = jnp.where(slot < rank[0], q, 0.0)
    basis_out[...] = q.T
    for copy in copies:
        copy.wait()
    h, l = split2(q)
    total = None
    for i in range(NY):
        hs, ls = h[:, i * t : (i + 1) * t], l[:, i * t : (i + 1) * t]
        by_hi = dot(jnp.concatenate([hs, ls], 0), hi[i], 1, 0)
        term = by_hi[:n] + (by_hi[n:] + dot(hs, lo[i], 1, 0))
        total = term if total is None else total + term
    core[...] = total
    own = n // NY
    for k, out in enumerate((core0, core1, core2, core3)):
        out[...] = core[pl.ds(pl.multiple_of(place[k] * own, 8), own), :]
    h, l = split2(total)
    param = jnp.zeros((PARAMS, PARAMS), F32)
    for s in range(total.shape[1] // PARAMS):
        hs, ls = h[:, s * PARAMS : (s + 1) * PARAMS], l[:, s * PARAMS : (s + 1) * PARAMS]
        cross = dot(hs, ls, 0, 0)
        param = param + (dot(hs, hs, 0, 0) + (cross + cross.T) + dot(ls, ls, 0, 0))
    param_out[...] = param


def solve(place, rank, pieces, start_basis, hi, lo, scale):
    time_all, ranks = start_basis.shape
    t, width = hi.shape[1:]
    struct = jax.ShapeDtypeStruct
    part = struct((ranks // NY, width), F32)
    vmem = pl.BlockSpec(memory_space=VMEM)
    smem = pl.BlockSpec(memory_space=SMEM)
    anywhere = pl.BlockSpec(memory_space=pl.ANY)

    def body(*refs):
        solve_kernel(*refs, scale=scale)

    return pl.pallas_call(
        body,
        out_shape=(struct((time_all, ranks), F32), part, part, part, part, struct((PARAMS, PARAMS), F32)),
        in_specs=[smem, smem] + [vmem] * 9 + [anywhere] * 2,
        out_specs=[vmem] * 6,
        scratch_shapes=[
            VMEM((len(PAIRS) * t, t), F32),
            VMEM((time_all, time_all), BF16),
            VMEM((time_all, time_all), BF16),
            VMEM((time_all, time_all), BF16),
            VMEM(hi.shape, BF16),
            VMEM(lo.shape, BF16),
            VMEM((ranks, 2 * ranks), F32),
            VMEM((ranks, width), F32),
            pltpu.SemaphoreType.DMA((2,)),
        ],
        compiler_params=pltpu.CompilerParams(vmem_limit_bytes=48 * 2**20),
        cost_estimate=pl.CostEstimate(flops=8 * 10**9, bytes_accessed=9 * 2**20, transcendentals=0),
        name="solve",
    )(place, rank, *pieces, start_basis, hi, lo)


def join_kernel(place, p0, p1, p2, p3, out):
    width = p0.shape[1]
    for k, piece in enumerate((p0, p1, p2, p3)):
        out[:, pl.ds(pl.multiple_of(place[k] * width, 128), width)] = piece[...]


def join_columns(place, pieces):
    rows, width = pieces[0].shape
    return pl.pallas_call(
        join_kernel,
        out_shape=jax.ShapeDtypeStruct((rows, NY * width), F32),
        in_specs=[pl.BlockSpec(memory_space=SMEM)] + [pl.BlockSpec(memory_space=VMEM)] * 4,
        out_specs=pl.BlockSpec(memory_space=VMEM),
        name="join_columns",
    )(place, *pieces)


def take(v, i):
    return lax.dynamic_index_in_dim(v, i, 0, keepdims=False)


def scatter_sum(v, me, move):
    got = [move(take(v, (me + k) % NX), k) for k in (1, 3, 2)]
    return take(v, me) + got[0] + got[1] + got[2]


def exchange_sum(v, move):
    got = [move(v, k) for k in (1, 3, 2)]
    return v + got[0] + got[1] + got[2]


def gather(v, move):
    got = {k: move(v, k) for k in (1, 3, 2)}
    return [v, got[1], got[2], got[3]]


def local(slab, start_basis, time_rank):
    rest_count = lax.axis_size("rest")
    time_local, columns_local = slab.shape
    columns_all = columns_local * rest_count
    width = columns_local // NY
    ranks = start_basis.shape[1]
    me_y = lax.axis_index("tm")
    rest = lax.axis_index("rest")
    core_id, me_z, me_x = rest % 2, (rest // 2) % NZ, rest // (2 * NZ)
    first_me = jnp.where(core_id == 0, me_x, me_z)
    second_me = jnp.where(core_id == 0, me_z, me_x)
    four = jnp.arange(NY, dtype=jnp.int32)

    def columns(k):
        return lax.dynamic_slice_in_dim(slab, (me_y + k) % NY * width, width, 1)

    got = {k: along_y(columns(k), k) for k in (1, 3, 2)}
    parts = [columns(0), got[1], got[2], got[3]]
    source_y = (me_y - four) % NY
    pairs = jnp.array(PAIRS, jnp.int32).reshape(2, HALF * 2)
    table = jnp.concatenate([source_y, take(pairs, 1 - core_id), take(pairs, core_id)])
    send, keep, hi, lo = partial_gram(table, parts)

    rows = HALF * time_local // (NX * NZ)
    v = (keep + along_core(send)).reshape(NX, NZ, rows, time_local)
    v = scatter_sum(v, first_me, lambda u, k: along_xz(u, k, True))
    v = scatter_sum(v, second_me, lambda u, k: along_xz(u, k, False))
    v = exchange_sum(v, along_y)
    v = jnp.stack(gather(v, lambda u, k: along_xz(u, k, False)))
    pieces = gather(v, lambda u, k: along_xz(u, k, True))
    pieces = pieces + [along_core(piece) for piece in pieces]

    def chunk(core, first, second):
        k, j = four[:, None], four[None, :]
        return ((core * NX + (first - k) % NX) * NZ + (second - j) % NZ).reshape(-1)

    place = jnp.concatenate(
        [(me_y + four) % NY, chunk(core_id, first_me, second_me), chunk(1 - core_id, second_me, first_me)]
    )
    basis, *cores, param = solve(place, time_rank, pieces, start_basis, hi, lo, 1.0 / columns_all)

    param = param + along_core(param)
    param = exchange_sum(param, lambda u, k: along_xz(u, k, True))
    param = exchange_sum(param, lambda u, k: along_xz(u, k, False))
    param = exchange_sum(param, along_y)
    space_all = columns_local // PARAMS * rest_count
    param_gram = param / float(ranks * space_all)

    mine = {k: along_y(cores[k], k) for k in (1, 3, 2)}
    core = join_columns(source_y, [cores[0], mine[1], mine[2], mine[3]])
    return (basis, core, param_gram)


def solution(mesh):
    in_specs = (P("tm", "rest"), P(), P())
    out_specs = (P(), P("tm", "rest"), P())
    return jax.shard_map(local, mesh=mesh, in_specs=in_specs, out_specs=out_specs, check_vma=False)
```

```python
import jax
import jax.numpy as jnp
from jax import lax
from jax.experimental import pallas as pl
from jax.experimental.pallas import tpu as pltpu
from jax.sharding import PartitionSpec as P

F32, BF16 = jnp.float32, jnp.bfloat16
PARAMS = 128
ITERS = 3
NY, NX, NZ = 4, 4, 4
VMEM, SMEM = pltpu.VMEM, pltpu.SMEM


def rest_index(x, z, c):
    return (x * NZ + z) * 2 + c


def along_y(v, k):
    return lax.ppermute(v, "tm", [(i, (i + k) % NY) for i in range(NY)])


def along_core(v):
    return lax.ppermute(v, "rest", [(i, i ^ 1) for i in range(2 * NX * NZ)])


def along_xz(v, k, first):
    perm = []
    for x in range(NX):
        for z in range(NZ):
            for c in range(2):
                if (c == 0) == first:
                    to = rest_index((x + k) % NX, z, c)
                else:
                    to = rest_index(x, (z + k) % NZ, c)
                perm.append((rest_index(x, z, c), to))
    return lax.ppermute(v, "rest", perm)


def split2(v):
    hi = v.astype(BF16)
    return hi, (v - hi.astype(F32)).astype(BF16)


def split3(v):
    hi = v.astype(BF16)
    rest = v - hi.astype(F32)
    mid = rest.astype(BF16)
    return hi, mid, (rest - mid.astype(F32)).astype(BF16)


def dot(a, b, ca, cb):
    return lax.dot_general(a, b, (((ca,), (cb,)), ((), ())), preferred_element_type=F32)


def product(hl, i, j, core, out):
    half = hl.shape[2] // 2
    send = pl.ds(pl.multiple_of((1 - core) * half, half), half)
    keep = pl.ds(pl.multiple_of(core * half, half), half)
    left = jnp.concatenate([hl[i, 0, send, :], hl[i, 0, keep, :], hl[i, 1, send, :], hl[i, 1, keep, :]], 0)
    by_h, by_l = dot(left, hl[j, 0], 1, 1), dot(left, hl[j, 1], 1, 1)
    out[0][...] = by_h[:half] + (by_h[2 * half : 3 * half] + by_l[:half] + by_l[2 * half : 3 * half])
    out[1][...] = by_h[half : 2 * half] + (by_h[3 * half :] + by_l[half : 2 * half] + by_l[3 * half :])


def own_kernel(table, slab, send, keep, hl_out, hl):
    h, l = split2(slab[...])
    hl[0, 0], hl[0, 1] = h, l
    width = hl_out.shape[2]
    mine = pl.ds(pl.multiple_of(table[1] * width, 128), width)
    hl_out[0], hl_out[1] = hl[0, 0, :, mine], hl[0, 1, :, mine]
    product(hl, 0, 0, table[0], (send, keep))


def early_kernel(table, w1, w3, hl0, send0, keep0, send, keep, hl1, hl3, hl, sem):
    copy = pltpu.make_async_copy(hl0, hl.at[0], sem)
    copy.start()
    for w, out, d in ((w1, hl3, 3), (w3, hl1, 1)):
        h, l = split2(w[...])
        out[0], out[1] = h, l
        hl[d, 0], hl[d, 1] = h, l
    send[0], keep[0] = send0[...], keep0[...]
    copy.wait()
    for n in range(3):
        product(hl, table[2 + 2 * n], table[3 + 2 * n], table[0], (send.at[n + 1], keep.at[n + 1]))


def late_kernel(table, w2, hl0, hl1, hl3, send, keep, hl2, hl, sem):
    copies = [pltpu.make_async_copy(x, hl.at[d], sem.at[d]) for x, d in ((hl0, 0), (hl3, 3), (hl1, 1))]
    for copy in copies:
        copy.start()
    h, l = split2(w2[...])
    hl2[0], hl2[1] = h, l
    hl[2, 0], hl[2, 1] = h, l
    for n in range(3):
        copies[n].wait()
        product(hl, table[8 + 2 * n], table[9 + 2 * n], table[0], (send.at[n], keep.at[n]))


def gram_call(kernel, name, table, vmem_args, any_args, more_args, blocks, wide, halves, cols):
    rows = 256
    struct = jax.ShapeDtypeStruct
    vmem, anywhere = pl.BlockSpec(memory_space=VMEM), pl.BlockSpec(memory_space=pl.ANY)
    half = struct((blocks, rows // 2, rows) if blocks else (rows // 2, rows), F32)
    scratch = [VMEM((4 if any_args else 1, 2, rows, wide), BF16)]
    if any_args:
        scratch.append(pltpu.SemaphoreType.DMA((4,)) if len(any_args) > 1 else pltpu.SemaphoreType.DMA)
    return pl.pallas_call(
        kernel,
        out_shape=[half, half] + [struct((2, rows, cols), BF16)] * halves,
        in_specs=[pl.BlockSpec(memory_space=SMEM)] + [vmem] * len(vmem_args) + [anywhere] * len(any_args) + [vmem] * len(more_args),
        out_specs=[vmem] * (2 + halves),
        scratch_shapes=scratch,
        compiler_params=pltpu.CompilerParams(vmem_limit_bytes=24 * 2**20),
        cost_estimate=pl.CostEstimate(
            flops=8 * rows * rows * wide * max(blocks, 1), bytes_accessed=6 * 2**20, transcendentals=0
        ),
        name=name,
    )(table, *vmem_args, *any_args, *more_args)


def row_of(v, k):
    return jnp.broadcast_to(v[k : k + 1, :], v.shape)


def cholesky_inverse(work):
    n = work.shape[0]
    r = lax.broadcasted_iota(jnp.int32, (n, n), 0)
    c = lax.broadcasted_iota(jnp.int32, (n, n), 1)
    work[:, n:] = (r == c).astype(F32)
    row = lax.broadcasted_iota(jnp.int32, (8, n), 0)
    panels = []
    for p in range(n // 8):
        left, right = work[8 * p : 8 * p + 8, :n], work[8 * p : 8 * p + 8, n:]
        column = [jnp.broadcast_to(left[:, 8 * p + j : 8 * p + j + 1], (8, n)) for j in range(8)]
        scale = jnp.zeros((8, n), F32)
        for k in range(8):
            pivot = row_of(column[k], k)
            factor = jnp.where(row > k, column[k] * (1.0 / pivot), 0.0)
            scale = jnp.where(row == k, lax.rsqrt(pivot), scale)
            for j in range(k + 1, 8):
                column[j] = column[j] - factor * row_of(column[j], k)
            if k < 7:
                left = left - factor * row_of(left, k)
                right = right - factor * row_of(right, k)
        left, right = left * scale, right * scale
        panels.append(right)
        if p < n // 8 - 1:
            h, m, l = split3(jnp.concatenate([left, right], 1))
            lh, lm, ll = h[:, :n], m[:, :n], l[:, :n]
            work[...] = work[...] - dot(
                jnp.concatenate([lh, lh, lm, lm, lh, ll], 0), jnp.concatenate([h, m, h, m, l, h], 0), 0, 0
            )
    return jnp.concatenate(panels, 0)


def solve_kernel(place, rank, *refs, scale):
    pieces, start, hl_in = refs[:8], refs[8], refs[9:13]
    basis_out, core0, core1, core2, core3, param_out = refs[13:19]
    packed, gh, gm, gl, hl, work, core, qhl, sem = refs[19:]
    copies = [pltpu.make_async_copy(x, hl.at[d], sem.at[d]) for d, x in enumerate(hl_in)]
    for copy in copies:
        copy.start()
    blocks, rows, t = pieces[0].shape
    for n, piece in enumerate(pieces):
        mine = place[12] if n < NX else 1 - place[12]
        at = pl.multiple_of(mine * (t // 2) + place[NY + n] * rows, rows)
        packed[:, pl.ds(at, rows), :] = piece[...]
    for n in range(blocks):
        i, j = place[13 + n], place[13 + blocks + n]
        block = packed[n] * scale
        for k, g in enumerate(split3(block)):
            (gh, gm, gl)[k][i, :, pl.ds(pl.multiple_of(j * t, t), t)] = g
        if n < 6:
            for k, g in enumerate(split3(block.T)):
                (gh, gm, gl)[k][j, :, pl.ds(pl.multiple_of(i * t, t), t)] = g

    q = start[...].T
    n = q.shape[0]
    for _ in range(ITERS):
        h, m, l = split3(q)
        by_h = dot(jnp.concatenate([h, m, l], 0), gh[...].reshape(NY * t, NY * t), 1, 0)
        by_m = dot(jnp.concatenate([h, m], 0), gm[...].reshape(NY * t, NY * t), 1, 0)
        by_l = dot(h, gl[...].reshape(NY * t, NY * t), 1, 0)
        image = by_h[:n] + ((by_h[n : 2 * n] + by_m[:n]) + (by_h[2 * n :] + by_m[n:] + by_l))
        h, m, l = split3(image)
        by_h = dot(jnp.concatenate([h, m, l], 0), h, 1, 1)
        small = by_h[n : 2 * n] + by_h[2 * n :]
        work[:, :n] = by_h[:n] + ((small + small.T) + dot(m, m, 1, 1))
        ih, im, il = split3(cholesky_inverse(work))
        by_h = dot(jnp.concatenate([ih, im, il], 0), h, 1, 0)
        by_m = dot(jnp.concatenate([ih, im], 0), m, 1, 0)
        q = by_h[:n] + ((by_h[n : 2 * n] + by_m[:n]) + (by_h[2 * n :] + by_m[n:] + dot(ih, l, 1, 0)))

    slot = lax.broadcasted_iota(jnp.int32, q.shape, 0)
    q = jnp.where(slot < rank[0], q, 0.0)
    basis_out[...] = q.T
    qhl[0], qhl[1] = split2(q)
    total = None
    for d in range(NY):
        copies[d].wait()
        at = pl.ds(pl.multiple_of(place[d] * t, t), t)
        hs, ls = qhl[0, :, at], qhl[1, :, at]
        by_hi = dot(jnp.concatenate([hs, ls], 0), hl[d, 0], 1, 0)
        term = by_hi[:n] + (by_hi[n:] + dot(hs, hl[d, 1], 1, 0))
        total = term if total is None else total + term
    core[...] = total
    own = n // NY
    for k, out in enumerate((core0, core1, core2, core3)):
        out[...] = core[pl.ds(pl.multiple_of(place[k] * own, 8), own), :]
    h, l = split2(total)
    param = jnp.zeros((PARAMS, PARAMS), F32)
    for s in range(total.shape[1] // PARAMS):
        hs, ls = h[:, s * PARAMS : (s + 1) * PARAMS], l[:, s * PARAMS : (s + 1) * PARAMS]
        cross = dot(hs, ls, 0, 0)
        param = param + (dot(hs, hs, 0, 0) + (cross + cross.T) + dot(ls, ls, 0, 0))
    param_out[...] = param


def solve(place, rank, pieces, start_basis, hls, scale):
    time_all, ranks = start_basis.shape
    blocks, _, t = pieces[0].shape
    width = hls[0].shape[2]
    struct = jax.ShapeDtypeStruct
    part = struct((ranks // NY, width), F32)
    vmem = pl.BlockSpec(memory_space=VMEM)
    smem = pl.BlockSpec(memory_space=SMEM)
    anywhere = pl.BlockSpec(memory_space=pl.ANY)

    def body(*refs):
        solve_kernel(*refs, scale=scale)

    return pl.pallas_call(
        body,
        out_shape=(struct((time_all, ranks), F32), part, part, part, part, struct((PARAMS, PARAMS), F32)),
        in_specs=[smem, smem] + [vmem] * 9 + [anywhere] * 4,
        out_specs=[vmem] * 6,
        scratch_shapes=[
            VMEM((blocks, t, t), F32),
            VMEM((NY, t, time_all), BF16),
            VMEM((NY, t, time_all), BF16),
            VMEM((NY, t, time_all), BF16),
            VMEM((NY, 2, t, width), BF16),
            VMEM((ranks, 2 * ranks), F32),
            VMEM((ranks, width), F32),
            VMEM((2, ranks, time_all), BF16),
            pltpu.SemaphoreType.DMA((NY,)),
        ],
        compiler_params=pltpu.CompilerParams(vmem_limit_bytes=36 * 2**20),
        cost_estimate=pl.CostEstimate(flops=8 * 10**9, bytes_accessed=9 * 2**20, transcendentals=0),
        name="solve",
    )(place, rank, *pieces, start_basis, *hls)


def join_kernel(place, p0, p1, p2, p3, out):
    width = p0.shape[1]
    for k, piece in enumerate((p0, p1, p2, p3)):
        out[:, pl.ds(pl.multiple_of(place[k] * width, 128), width)] = piece[...]


def join_columns(place, pieces):
    rows, width = pieces[0].shape
    return pl.pallas_call(
        join_kernel,
        out_shape=jax.ShapeDtypeStruct((rows, NY * width), F32),
        in_specs=[pl.BlockSpec(memory_space=SMEM)] + [pl.BlockSpec(memory_space=VMEM)] * 4,
        out_specs=pl.BlockSpec(memory_space=VMEM),
        name="join_columns",
    )(place, *pieces)


def scatter_sum(v, me, move):
    v = v.reshape(v.shape[0], NX, v.shape[1] // NX, v.shape[2])

    def slot(k):
        return lax.dynamic_index_in_dim(v, (me + k) % NX, 1, keepdims=False)

    got = [move(slot(k), k) for k in (1, 3, 2)]
    return slot(0) + got[0] + got[1] + got[2]


def exchange_sum(v, move):
    got = [move(v, k) for k in (1, 3, 2)]
    return v + got[0] + got[1] + got[2]


def gather(v, move):
    got = {k: move(v, k) for k in (1, 3, 2)}
    return [v, got[1], got[2], got[3]]


def local(slab, start_basis, time_rank):
    rest_count = lax.axis_size("rest")
    time_local, columns_local = slab.shape
    columns_all = columns_local * rest_count
    width = columns_local // NY
    ranks = start_basis.shape[1]
    me_y = lax.axis_index("tm")
    rest = lax.axis_index("rest")
    core_id, me_z, me_x = rest % 2, (rest // 2) % NZ, rest // (2 * NZ)
    first_me = jnp.where(core_id == 0, me_x, me_z)
    second_me = jnp.where(core_id == 0, me_z, me_x)
    four = jnp.arange(NY, dtype=jnp.int32)

    def columns(v, k):
        return lax.dynamic_slice_in_dim(v, (me_y + k) % NY * width, width, 1)

    v, got = slab, {}
    for k in (1, 3, 2):
        out = columns(v, k)
        v, out = lax.optimization_barrier((v, out))
        got[k] = along_y(out, k)
    source_y, ahead = (me_y - four) % NY, (me_y + four) % NY

    def low_first(i, j):
        swap = ahead[i] > ahead[j]
        return [jnp.where(swap, j, i), jnp.where(swap, i, j)]

    fixed = [jnp.int32(n) for n in (0, 1, 3, 0, 2, 3, 1, 2)]
    table = jnp.stack(
        [core_id, me_y] + fixed[:4] + low_first(3, 1) + low_first(0, 2) + fixed[4:]
    ).astype(jnp.int32)

    def plane_sum(send, keep):
        u = keep + along_core(send)
        u = scatter_sum(u, first_me, lambda w, k: along_xz(w, k, True))
        return exchange_sum(u, lambda w, k: along_xz(w, k, False))

    send0, keep0, hl0 = gram_call(own_kernel, "own_gram", table, [slab], [], [], 0, columns_local, 1, width)
    send, keep, hl1, hl3 = gram_call(
        early_kernel, "early_gram", table, [got[1], got[3]], [hl0], [send0, keep0], 4, width, 2, width
    )
    early = plane_sum(send, keep)
    early, w2 = lax.optimization_barrier((early, got[2]))
    send, keep, hl2 = gram_call(late_kernel, "late_gram", table, [w2], [hl0, hl1, hl3], [], 3, width, 1, width)
    late = plane_sum(send, keep)

    v = jnp.concatenate([early, late])
    got = {k: along_y(v, k) for k in (1, 3, 2)}
    at = [v, got[3], got[2], got[1]]

    def term(d, n):
        return at[d % NY][n]

    v = jnp.stack(
        [term(d, 1) + term(d + 1, 2) + term(d + 2, 5) + term(d + 3, 6) for d in range(NY)]
        + [term(d, 4) + term(d + 2, 4) + term(d + 1, 3) + term(d + 3, 3) for d in range(2)]
        + [term(d, 0) for d in range(NY)]
    )
    pieces = gather(v, lambda u, k: along_xz(u, k, True))
    pieces = pieces + [along_core(piece) for piece in pieces]
    rows_of = [ahead[d] for d in range(NY)] + [jnp.minimum(ahead[d], ahead[d + 2]) for d in range(2)]
    cols_of = [ahead[(d + 1) % NY] for d in range(NY)] + [jnp.maximum(ahead[d], ahead[d + 2]) for d in range(2)]
    place = jnp.concatenate(
        [ahead, (first_me - four) % NX, (second_me - four) % NX]
        + [jnp.stack([core_id] + rows_of + list(ahead) + cols_of + list(ahead))]
    ).astype(jnp.int32)
    basis, *cores, param = solve(place, time_rank, pieces, start_basis, [hl0, hl1, hl2, hl3], 1.0 / columns_all)

    param = param + along_core(param)
    param = exchange_sum(param, lambda u, k: along_xz(u, k, True))
    param = exchange_sum(param, lambda u, k: along_xz(u, k, False))
    param = exchange_sum(param, along_y)
    space_all = columns_local // PARAMS * rest_count
    param_gram = param / float(ranks * space_all)

    mine = {k: along_y(cores[k], k) for k in (1, 3, 2)}
    core = join_columns(source_y, [cores[0], mine[1], mine[2], mine[3]])
    return (basis, core, param_gram)


def solution(mesh):
    in_specs = (P("tm", "rest"), P(), P())
    out_specs = (P(), P("tm", "rest"), P())
    return jax.shard_map(local, mesh=mesh, in_specs=in_specs, out_specs=out_specs, check_vma=False)
```

```python
import jax
import jax.numpy as jnp
from jax import lax
from jax.experimental import pallas as pl
from jax.experimental.pallas import tpu as pltpu
from jax.sharding import PartitionSpec as P

F32, BF16 = jnp.float32, jnp.bfloat16
PARAMS = 128
ITERS = 3
COST = {"own_gram": 10**9, "early_gram": 10**9, "late_gram": 2 * 10**10}
NY, NX, NZ = 4, 4, 4
VMEM, SMEM, HBM = pltpu.VMEM, pltpu.SMEM, pltpu.HBM


def rest_index(x, z, c):
    return (x * NZ + z) * 2 + c


def along_y(v, k):
    return lax.ppermute(v, "tm", [(i, (i + k) % NY) for i in range(NY)])


def along_core(v):
    return lax.ppermute(v, "rest", [(i, i ^ 1) for i in range(2 * NX * NZ)])


def along_xz(v, k, first):
    perm = []
    for x in range(NX):
        for z in range(NZ):
            for c in range(2):
                if (c == 0) == first:
                    to = rest_index((x + k) % NX, z, c)
                else:
                    to = rest_index(x, (z + k) % NZ, c)
                perm.append((rest_index(x, z, c), to))
    return lax.ppermute(v, "rest", perm)


def position():
    me_y, rest = lax.axis_index("tm"), lax.axis_index("rest")
    core, z, x = lax.rem(rest, 2), lax.rem(lax.div(rest, 2), NZ), lax.div(rest, 2 * NZ)
    return me_y, core, jnp.where(core == 0, x, z), jnp.where(core == 0, z, x)


def around(i, k):
    return lax.rem(i + k, 4)


def low_first(me, i, j):
    swap = around(me, i) > around(me, j)
    return jnp.where(swap, j, i), jnp.where(swap, i, j)


def split2(v):
    hi = v.astype(BF16)
    return hi, (v - hi.astype(F32)).astype(BF16)


def split3(v):
    hi = v.astype(BF16)
    rest = v - hi.astype(F32)
    mid = rest.astype(BF16)
    return hi, mid, (rest - mid.astype(F32)).astype(BF16)


def dot(a, b, ca, cb):
    return lax.dot_general(a, b, (((ca,), (cb,)), ((), ())), preferred_element_type=F32)


def product(hl, i, j, core, out):
    h, l = hl.at[i], hl.at[j]
    total = dot(h[0], l[0], 1, 1) + (dot(h[1], l[0], 1, 1) + dot(h[0], l[1], 1, 1) + dot(h[1], l[1], 1, 1))
    half = total.shape[0] // 2
    out[0][...] = jnp.where(core == 0, total[half:], total[:half])
    out[1][...] = jnp.where(core == 0, total[:half], total[half:])


def own_kernel(slab, send, keep, hl_out, across, hl, sem):
    me_y, core, _, _ = position()
    h, l = split2(slab[...])
    hl[0, 0], hl[0, 1] = h, l
    width = hl_out.shape[2]
    mine = pl.ds(pl.multiple_of(me_y * width, 128), width)
    theirs = pl.ds(pl.multiple_of(around(me_y, 2) * width, 128), width)
    outs = [
        pltpu.make_async_copy(hl.at[0, :, :, mine], hl_out, sem.at[0]),
        pltpu.make_async_copy(slab.at[:, theirs], across, sem.at[1]),
    ]
    for out in outs:
        out.start()
    product(hl, 0, 0, core, (send, keep))
    for out in outs:
        out.wait()


def slices_kernel(slab, ahead, behind, sem):
    me_y = lax.axis_index("tm")
    width = ahead.shape[1]
    outs = []
    for n, (k, out) in enumerate(((1, ahead), (3, behind))):
        at = pl.ds(pl.multiple_of(around(me_y, k) * width, 128), width)
        outs.append(pltpu.make_async_copy(slab.at[:, at], out, sem.at[n]))
    for out in outs:
        out.start()
    for out in outs:
        out.wait()


def slices(slab):
    out = jax.ShapeDtypeStruct((slab.shape[0], slab.shape[1] // NY), F32)
    hbm = pl.BlockSpec(memory_space=HBM)
    return pl.pallas_call(
        slices_kernel,
        out_shape=[out, out],
        in_specs=[hbm],
        out_specs=[pl.BlockSpec(memory_space=VMEM)] * 2,
        scratch_shapes=[pltpu.SemaphoreType.DMA((2,))],
        compiler_params=pltpu.CompilerParams(vmem_limit_bytes=56 * 2**20),
        name="slices",
    )(slab)


def early_kernel(w1, w3, send0, keep0, hl0, send, keep, hl1, hl3, hl, sem):
    me_y, core, _, _ = position()
    copy = pltpu.make_async_copy(hl0, hl.at[0], sem.at[0])
    copy.start()
    for w, d in ((w1, 3), (w3, 1)):
        h, l = split2(w[...])
        hl[d, 0], hl[d, 1] = h, l
    outs = [pltpu.make_async_copy(hl.at[d], x, sem.at[d]) for x, d in ((hl1, 1), (hl3, 3))]
    for out in outs:
        out.start()
    send[0], keep[0] = send0[...], keep0[...]
    copy.wait()
    for n, (i, j) in enumerate(((0, 1), (3, 0), low_first(me_y, 3, 1))):
        product(hl, i, j, core, (send.at[n + 1], keep.at[n + 1]))
    for out in outs:
        out.wait()


def late_kernel(w2, hl0, hl1, hl3, send, keep, hl, sem):
    me_y, core, _, _ = position()
    copies = [pltpu.make_async_copy(x, hl.at[d], sem.at[d]) for x, d in ((hl0, 0), (hl3, 3), (hl1, 1))]
    for copy in copies:
        copy.start()
    h, l = split2(w2[...])
    hl[2, 0], hl[2, 1] = h, l
    for n, (i, j) in enumerate((low_first(me_y, 0, 2), (2, 3), (1, 2))):
        copies[n].wait()
        product(hl, i, j, core, (send.at[n], keep.at[n]))


def gram_call(kernel, name, vmem_args, hbm_args, blocks, wide, halves, cols):
    rows = 256
    struct = jax.ShapeDtypeStruct
    vmem, hbm = pl.BlockSpec(memory_space=VMEM), pl.BlockSpec(memory_space=HBM)
    half = struct((blocks, rows // 2, rows) if blocks else (rows // 2, rows), F32)
    slots = NY if hbm_args else 1
    return pl.pallas_call(
        kernel,
        out_shape=[half, half] + [struct((2, rows, cols), BF16)] * halves + [struct((rows, cols), F32)] * (1 - slots // NY),
        in_specs=[vmem] * len(vmem_args) + [hbm] * len(hbm_args),
        out_specs=[vmem] * 2 + [hbm] * (halves + 1 - slots // NY),
        scratch_shapes=[VMEM((slots, 2, rows, wide), BF16), pltpu.SemaphoreType.DMA((NY,))],
        compiler_params=pltpu.CompilerParams(vmem_limit_bytes=16 * 2**20),
        cost_estimate=pl.CostEstimate(flops=COST.get(name, 10**9), bytes_accessed=1000, transcendentals=0),
        name=name,
    )(*vmem_args, *hbm_args)


def row_of(v, k):
    return jnp.broadcast_to(v[k : k + 1, :], v.shape)


def cholesky_inverse(work):
    n = work.shape[0]
    panels = n // 8
    r = lax.broadcasted_iota(jnp.int32, (n, n), 0)
    c = lax.broadcasted_iota(jnp.int32, (n, n), 1)
    work[:, n:] = (r == c).astype(F32)
    row = lax.broadcasted_iota(jnp.int32, (8, n), 0)
    left, right = {}, {}

    def load(t):
        left[t], right[t] = work[8 * t : 8 * t + 8, :n], work[8 * t : 8 * t + 8, n:]

    def columns(t, p):
        return [jnp.broadcast_to(left[t][:, 8 * p + j : 8 * p + j + 1], (8, n)) for j in range(8)]

    for t in range(2):
        load(t)
    column = columns(0, 0)
    for p in range(panels):
        first = p - p % 2
        if p == first:
            for t in range(first + 2, min(first + 4, panels)):
                load(t)
        below = range(p + 1, min(first + 4, panels))
        entries = {t: columns(t, p) for t in below}
        ahead = columns(p + 1, p + 1) if below else None
        scale = jnp.zeros((8, n), F32)
        for k in range(8):
            pivot = row_of(column[k], k)
            inverse = 1.0 / pivot
            scale = jnp.where(row == k, lax.rsqrt(pivot), scale)
            factor = jnp.where(row > k, column[k] * inverse, 0.0)
            across = [row_of(column[j], k) for j in range(k + 1, 8)]
            for j in range(k + 1, 8):
                column[j] = column[j] - factor * across[j - k - 1]
            left_k, right_k = row_of(left[p], k), row_of(right[p], k)
            left[p], right[p] = left[p] - factor * left_k, right[p] - factor * right_k
            for t in below:
                factor = entries[t][k] * inverse
                if t == p + 1:
                    ahead = [ahead[j] - factor * row_of(entries[t][k], j) for j in range(8)]
                for j in range(k + 1, 8):
                    entries[t][j] = entries[t][j] - factor * across[j - k - 1]
                left[t], right[t] = left[t] - factor * left_k, right[t] - factor * right_k
        left[p], right[p] = left[p] * scale, right[p] * scale
        if p > first and first + 4 < panels:
            h, m, l = split3(jnp.concatenate([jnp.concatenate([left[t], right[t]], 1) for t in (first, p)], 0))
            lh, lm, ll = h[:, :n], m[:, :n], l[:, :n]
            update = dot(jnp.concatenate([lh, lh, lm, lm, lh, ll], 0), jnp.concatenate([h, m, h, m, l, h], 0), 0, 0)
            start = 8 * (first + 4)
            work[start:, :] = work[start:, :] - update[start:]
        column = ahead
    return jnp.concatenate([right[p] for p in range(panels)], 0)


def solve_kernel(rank, *refs, scale):
    me_y, core_id, first, second = position()
    pieces, start, hl_in = refs[:8], refs[8], refs[9:13]
    basis_out, core0, core1, core2, core3, param_out = refs[13:19]
    packed, gh, gm, gl, hl, last, work, core, qhl, sem = refs[19:]
    ends = ((hl_in[0], hl.at[0]), (hl_in[1], hl.at[1]), (hl_in[3], last), (hl_in[2], hl.at[3]))
    copies = [pltpu.make_async_copy(x, y, sem.at[d]) for d, (x, y) in enumerate(ends)]
    for copy in copies:
        copy.start()
    blocks, rows, t = pieces[0].shape
    for n, piece in enumerate(pieces):
        half, base = (core_id, first) if n < NX else (1 - core_id, second)
        at = pl.multiple_of(half * (t // 2) + around(base, NX - n % NX) * rows, rows)
        packed[:, pl.ds(at, rows), :] = piece[...]
    for n, (i, j) in enumerate(
        [(around(me_y, d), around(me_y, d + 1)) for d in range(NY)]
        + [tuple(around(me_y, d) for d in low_first(me_y, e, e + 2)) for e in range(2)]
        + [(around(me_y, d), around(me_y, d)) for d in range(NY)]
    ):
        block = packed[n] * scale
        for k, g in enumerate(split3(block)):
            (gh, gm, gl)[k][i, :, pl.ds(pl.multiple_of(j * t, t), t)] = g
        if n < 6:
            for k, g in enumerate(split3(block.T)):
                (gh, gm, gl)[k][j, :, pl.ds(pl.multiple_of(i * t, t), t)] = g

    q = start[...].T
    n = q.shape[0]
    for _ in range(ITERS):
        h, m, l = split3(q)
        by_h = dot(jnp.concatenate([h, m, l], 0), gh[...].reshape(NY * t, NY * t), 1, 0)
        by_m = dot(jnp.concatenate([h, m], 0), gm[...].reshape(NY * t, NY * t), 1, 0)
        by_l = dot(h, gl[...].reshape(NY * t, NY * t), 1, 0)
        image = by_h[:n] + ((by_h[n : 2 * n] + by_m[:n]) + (by_h[2 * n :] + by_m[n:] + by_l))
        h, m, l = split3(image)
        by_h = dot(jnp.concatenate([h, m, l], 0), h, 1, 1)
        small = by_h[n : 2 * n] + by_h[2 * n :]
        work[:, :n] = by_h[:n] + ((small + small.T) + dot(m, m, 1, 1))
        ih, im, il = split3(cholesky_inverse(work))
        by_h = dot(jnp.concatenate([ih, im, il], 0), h, 1, 0)
        by_m = dot(jnp.concatenate([ih, im], 0), m, 1, 0)
        q = by_h[:n] + ((by_h[n : 2 * n] + by_m[:n]) + (by_h[2 * n :] + by_m[n:] + dot(ih, l, 1, 0)))

    slot = lax.broadcasted_iota(jnp.int32, q.shape, 0)
    q = jnp.where(slot < rank[0], q, 0.0)
    basis_out[...] = q.T
    qhl[0], qhl[1] = split2(q)
    total = None
    for d in range(NY):
        copies[d].wait()
        if d == 2:
            hl[2, 0], hl[2, 1] = split2(last[...])
        at = pl.ds(pl.multiple_of(around(me_y, d) * t, t), t)
        hs, ls = qhl[0, :, at], qhl[1, :, at]
        by_hi = dot(jnp.concatenate([hs, ls], 0), hl[d, 0], 1, 0)
        term = by_hi[:n] + (by_hi[n:] + dot(hs, hl[d, 1], 1, 0))
        total = term if total is None else total + term
    core[...] = total
    own = n // NY
    for k, out in enumerate((core0, core1, core2, core3)):
        out[...] = core[pl.ds(pl.multiple_of(around(me_y, k) * own, 8), own), :]
    h, l = split2(total)
    param = jnp.zeros((PARAMS, PARAMS), F32)
    for s in range(total.shape[1] // PARAMS):
        hs, ls = h[:, s * PARAMS : (s + 1) * PARAMS], l[:, s * PARAMS : (s + 1) * PARAMS]
        cross = dot(hs, ls, 0, 0)
        param = param + (dot(hs, hs, 0, 0) + (cross + cross.T) + dot(ls, ls, 0, 0))
    param_out[...] = param


def solve(rank, pieces, start_basis, hls, scale):
    time_all, ranks = start_basis.shape
    blocks, _, t = pieces[0].shape
    width = hls[0].shape[2]
    struct = jax.ShapeDtypeStruct
    part = struct((ranks // NY, width), F32)
    vmem = pl.BlockSpec(memory_space=VMEM)
    smem = pl.BlockSpec(memory_space=SMEM)
    hbm = pl.BlockSpec(memory_space=HBM)

    def body(*refs):
        solve_kernel(*refs, scale=scale)

    return pl.pallas_call(
        body,
        out_shape=(struct((time_all, ranks), F32), part, part, part, part, struct((PARAMS, PARAMS), F32)),
        in_specs=[smem] + [vmem] * 9 + [hbm] * 4,
        out_specs=[vmem] * 6,
        scratch_shapes=[
            VMEM((blocks, t, t), F32),
            VMEM((NY, t, time_all), BF16),
            VMEM((NY, t, time_all), BF16),
            VMEM((NY, t, time_all), BF16),
            VMEM((NY, 2, t, width), BF16),
            VMEM((t, width), F32),
            VMEM((ranks, 2 * ranks), F32),
            VMEM((ranks, width), F32),
            VMEM((2, ranks, time_all), BF16),
            pltpu.SemaphoreType.DMA((NY,)),
        ],
        compiler_params=pltpu.CompilerParams(vmem_limit_bytes=28 * 2**20),
        cost_estimate=pl.CostEstimate(flops=8 * 10**9, bytes_accessed=9 * 2**20, transcendentals=0),
        name="solve",
    )(rank, *pieces, start_basis, *hls)


def join_kernel(p0, p1, p2, p3, out):
    me_y = lax.axis_index("tm")
    width = p0.shape[1]
    for k, piece in enumerate((p0, p1, p2, p3)):
        out[:, pl.ds(pl.multiple_of(around(me_y, NY - k) * width, 128), width)] = piece[...]


def join_columns(pieces):
    rows, width = pieces[0].shape
    return pl.pallas_call(
        join_kernel,
        out_shape=jax.ShapeDtypeStruct((rows, NY * width), F32),
        in_specs=[pl.BlockSpec(memory_space=VMEM)] * 4,
        out_specs=pl.BlockSpec(memory_space=VMEM),
        compiler_params=pltpu.CompilerParams(vmem_limit_bytes=4 * 2**20),
        name="join_columns",
    )(*pieces)


def scatter_sum(v, me, move):
    v = v.reshape(v.shape[0], NX, v.shape[1] // NX, v.shape[2])

    def slot(k):
        return lax.dynamic_index_in_dim(v, (me + k) % NX, 1, keepdims=False)

    got = [move(slot(k), k) for k in (1, 3, 2)]
    return slot(0) + got[0] + got[1] + got[2]


def exchange_sum(v, move):
    got = [move(v, k) for k in (1, 3, 2)]
    return v + got[0] + got[1] + got[2]


def gather(v, move):
    got = {k: move(v, k) for k in (1, 3, 2)}
    return [v, got[1], got[2], got[3]]


def local(slab, start_basis, time_rank):
    rest_count = lax.axis_size("rest")
    columns_local = slab.shape[1]
    columns_all = columns_local * rest_count
    width = columns_local // NY
    ranks = start_basis.shape[1]
    _, _, first_me, _ = position()

    def scatter(send, keep):
        return scatter_sum(keep + along_core(send), first_me, lambda w, k: along_xz(w, k, True))

    def exchange(u):
        return exchange_sum(u, lambda w, k: along_xz(w, k, False))

    next_cols, last_cols = slices(slab)
    w1, w3 = along_y(next_cols, 1), along_y(last_cols, 3)
    send0, keep0, hl0, across = gram_call(own_kernel, "own_gram", [slab], [], 0, columns_local, 1, width)
    w1, w3, across = lax.optimization_barrier((w1, w3, across))
    w2 = along_y(across, 2)
    send, keep, hl1, hl3 = gram_call(early_kernel, "early_gram", [w1, w3, send0, keep0], [hl0], 4, width, 2, width)
    early = scatter(send, keep)
    early, w2 = lax.optimization_barrier((early, w2))
    early = exchange(early)
    send, keep = gram_call(late_kernel, "late_gram", [w2], [hl0, hl1, hl3], 3, width, 0, width)
    late = exchange(scatter(send, keep))
    v = jnp.concatenate([early, late])
    got = {k: along_y(v, k) for k in (1, 3, 2)}
    at = [v, got[3], got[2], got[1]]

    def term(d, n):
        return at[d % NY][n]

    v = jnp.stack(
        [term(d, 1) + term(d + 1, 2) + term(d + 2, 5) + term(d + 3, 6) for d in range(NY)]
        + [term(d, 4) + term(d + 2, 4) + term(d + 1, 3) + term(d + 3, 3) for d in range(2)]
        + [term(d, 0) for d in range(NY)]
    )
    pieces = gather(v, lambda u, k: along_xz(u, k, True))
    pieces = pieces + [along_core(piece) for piece in pieces]
    basis, *cores, param = solve(time_rank, pieces, start_basis, [hl0, hl1, hl3, w2], 1.0 / columns_all)

    mine = [cores[0]] + [along_y(cores[k], k) for k in (1, 2, 3)]
    param = param + along_core(param)
    param = exchange_sum(param, lambda u, k: along_xz(u, k, True))
    param = exchange_sum(param, lambda u, k: along_xz(u, k, False))
    param, mine = lax.optimization_barrier((param, mine))
    param = exchange_sum(param, along_y)
    space_all = columns_local // PARAMS * rest_count
    param_gram = param / float(ranks * space_all)
    core = join_columns(mine)
    return (basis, core, param_gram)


def solution(mesh):
    in_specs = (P("tm", "rest"), P(), P())
    out_specs = (P(), P("tm", "rest"), P())
    return jax.shard_map(local, mesh=mesh, in_specs=in_specs, out_specs=out_specs, check_vma=False)
```

```python
import jax
import jax.numpy as jnp
from jax import lax
from jax.experimental import pallas as pl
from jax.experimental.pallas import tpu as pltpu
from jax.sharding import PartitionSpec as P

F32, BF16 = jnp.float32, jnp.bfloat16
PARAMS = 128
ITERS = 3
HELD = 56
COST = {"own_gram": 10**9, "early_gram": 10**9, "late_gram": 2 * 10**10}
NY, NX, NZ = 4, 4, 4
VMEM, SMEM, HBM = pltpu.VMEM, pltpu.SMEM, pltpu.HBM


def rest_index(x, z, c):
    return (x * NZ + z) * 2 + c


def along_y(v, k):
    return lax.ppermute(v, "tm", [(i, (i + k) % NY) for i in range(NY)])


def along_core(v):
    return lax.ppermute(v, "rest", [(i, i ^ 1) for i in range(2 * NX * NZ)])


def along_xz(v, k, first):
    perm = []
    for x in range(NX):
        for z in range(NZ):
            for c in range(2):
                if (c == 0) == first:
                    to = rest_index((x + k) % NX, z, c)
                else:
                    to = rest_index(x, (z + k) % NZ, c)
                perm.append((rest_index(x, z, c), to))
    return lax.ppermute(v, "rest", perm)


def position():
    me_y, rest = lax.axis_index("tm"), lax.axis_index("rest")
    core, z, x = lax.rem(rest, 2), lax.rem(lax.div(rest, 2), NZ), lax.div(rest, 2 * NZ)
    return me_y, core, jnp.where(core == 0, x, z), jnp.where(core == 0, z, x)


def around(i, k):
    return lax.rem(i + k, 4)


def low_first(me, i, j):
    swap = around(me, i) > around(me, j)
    return jnp.where(swap, j, i), jnp.where(swap, i, j)


def split2(v):
    hi = v.astype(BF16)
    return hi, (v - hi.astype(F32)).astype(BF16)


def split3(v):
    hi = v.astype(BF16)
    rest = v - hi.astype(F32)
    mid = rest.astype(BF16)
    return hi, mid, (rest - mid.astype(F32)).astype(BF16)


def dot(a, b, ca, cb):
    return lax.dot_general(a, b, (((ca,), (cb,)), ((), ())), preferred_element_type=F32)


def product(hl, i, j, core, out):
    h, l = hl.at[i], hl.at[j]
    total = dot(h[0], l[0], 1, 1) + (dot(h[1], l[0], 1, 1) + dot(h[0], l[1], 1, 1) + dot(h[1], l[1], 1, 1))
    half = total.shape[0] // 2
    out[0][...] = jnp.where(core == 0, total[half:], total[:half])
    out[1][...] = jnp.where(core == 0, total[:half], total[half:])


def own_kernel(slab, send, keep, hl_out, across, hl, sem):
    me_y, core, _, _ = position()
    h, l = split2(slab[...])
    hl[0, 0], hl[0, 1] = h, l
    width = hl_out.shape[2]
    mine = pl.ds(pl.multiple_of(me_y * width, 128), width)
    theirs = pl.ds(pl.multiple_of(around(me_y, 2) * width, 128), width)
    outs = [
        pltpu.make_async_copy(hl.at[0, :, :, mine], hl_out, sem.at[0]),
        pltpu.make_async_copy(slab.at[:, theirs], across, sem.at[1]),
    ]
    for out in outs:
        out.start()
    product(hl, 0, 0, core, (send, keep))
    for out in outs:
        out.wait()


def slices_kernel(slab, ahead, behind, sem):
    me_y = lax.axis_index("tm")
    width = ahead.shape[1]
    outs = []
    for n, (k, out) in enumerate(((1, ahead), (3, behind))):
        at = pl.ds(pl.multiple_of(around(me_y, k) * width, 128), width)
        outs.append(pltpu.make_async_copy(slab.at[:, at], out, sem.at[n]))
    for out in outs:
        out.start()
    for out in outs:
        out.wait()


def slices(slab):
    out = jax.ShapeDtypeStruct((slab.shape[0], slab.shape[1] // NY), F32)
    hbm = pl.BlockSpec(memory_space=HBM)
    return pl.pallas_call(
        slices_kernel,
        out_shape=[out, out],
        in_specs=[hbm],
        out_specs=[pl.BlockSpec(memory_space=VMEM)] * 2,
        scratch_shapes=[pltpu.SemaphoreType.DMA((2,))],
        compiler_params=pltpu.CompilerParams(vmem_limit_bytes=56 * 2**20),
        name="slices",
    )(slab)


def early_kernel(w1, w3, send0, keep0, hl0, send, keep, hls, hl, sem):
    me_y, core, _, _ = position()
    copy = pltpu.make_async_copy(hl0, hl.at[0], sem.at[0])
    copy.start()
    for w, d in ((w1, 3), (w3, 1)):
        h, l = split2(w[...])
        hl[d, 0], hl[d, 1] = h, l
    outs = [pltpu.make_async_copy(hl.at[d], hls.at[d], sem.at[d]) for d in (1, 3, 0)]
    for out in outs[:2]:
        out.start()
    send[0], keep[0] = send0[...], keep0[...]
    copy.wait()
    outs[2].start()
    for n, (i, j) in enumerate(((0, 1), (3, 0), low_first(me_y, 3, 1))):
        product(hl, i, j, core, (send.at[n + 1], keep.at[n + 1]))
    for out in outs:
        out.wait()


def late_kernel(w2, hls, send, keep, hl, sem):
    me_y, core, _, _ = position()
    copies = [pltpu.make_async_copy(hls.at[d], hl.at[d], sem.at[d]) for d in (0, 3, 1)]
    for copy in copies:
        copy.start()
    h, l = split2(w2[...])
    hl[2, 0], hl[2, 1] = h, l
    for n, (i, j) in enumerate((low_first(me_y, 0, 2), (2, 3), (1, 2))):
        copies[n].wait()
        product(hl, i, j, core, (send.at[n], keep.at[n]))


def gram_call(kernel, name, vmem_args, hbm_args, blocks, wide, halves, cols):
    rows = 256
    struct = jax.ShapeDtypeStruct
    vmem, hbm = pl.BlockSpec(memory_space=VMEM), pl.BlockSpec(memory_space=HBM)
    half = struct((blocks, rows // 2, rows) if blocks else (rows // 2, rows), F32)
    slots = NY if hbm_args else 1
    return pl.pallas_call(
        kernel,
        out_shape=[half, half] + [struct((2, rows, cols) if blocks == 0 else (HELD, 2, rows, cols), BF16)] * halves + [struct((rows, cols), F32)] * (1 - slots // NY),
        in_specs=[vmem] * len(vmem_args) + [hbm] * len(hbm_args),
        out_specs=[vmem] * 2 + [hbm] * (halves + 1 - slots // NY),
        scratch_shapes=[VMEM((slots, 2, rows, wide), BF16), pltpu.SemaphoreType.DMA((NY,))],
        compiler_params=pltpu.CompilerParams(vmem_limit_bytes=16 * 2**20),
        cost_estimate=pl.CostEstimate(flops=COST.get(name, 10**9), bytes_accessed=1000, transcendentals=0),
        name=name,
    )(*vmem_args, *hbm_args)


def row_of(v, k):
    return jnp.broadcast_to(v[k : k + 1, :], v.shape)


def cholesky_inverse(work):
    n = work.shape[0]
    panels = n // 8
    r = lax.broadcasted_iota(jnp.int32, (n, n), 0)
    c = lax.broadcasted_iota(jnp.int32, (n, n), 1)
    work[:, n:] = (r == c).astype(F32)
    row = lax.broadcasted_iota(jnp.int32, (8, n), 0)
    left, right = {}, {}

    def load(t):
        left[t], right[t] = work[8 * t : 8 * t + 8, :n], work[8 * t : 8 * t + 8, n:]

    def columns(t, p):
        return [jnp.broadcast_to(left[t][:, 8 * p + j : 8 * p + j + 1], (8, n)) for j in range(8)]

    for t in range(2):
        load(t)
    column = columns(0, 0)
    for p in range(panels):
        first = p - p % 2
        if p == first:
            for t in range(first + 2, min(first + 4, panels)):
                load(t)
        below = range(p + 1, min(first + 4, panels))
        entries = {t: columns(t, p) for t in below}
        ahead = columns(p + 1, p + 1) if below else None
        scale = jnp.zeros((8, n), F32)
        for k in range(8):
            pivot = row_of(column[k], k)
            inverse = 1.0 / pivot
            scale = jnp.where(row == k, lax.rsqrt(pivot), scale)
            factor = jnp.where(row > k, column[k] * inverse, 0.0)
            across = [row_of(column[j], k) for j in range(k + 1, 8)]
            for j in range(k + 1, 8):
                column[j] = column[j] - factor * across[j - k - 1]
            left_k, right_k = row_of(left[p], k), row_of(right[p], k)
            left[p], right[p] = left[p] - factor * left_k, right[p] - factor * right_k
            for t in below:
                factor = entries[t][k] * inverse
                if t == p + 1:
                    ahead = [ahead[j] - factor * row_of(entries[t][k], j) for j in range(8)]
                for j in range(k + 1, 8):
                    entries[t][j] = entries[t][j] - factor * across[j - k - 1]
                left[t], right[t] = left[t] - factor * left_k, right[t] - factor * right_k
        left[p], right[p] = left[p] * scale, right[p] * scale
        if p > first and first + 4 < panels:
            h, m, l = split3(jnp.concatenate([jnp.concatenate([left[t], right[t]], 1) for t in (first, p)], 0))
            lh, lm, ll = h[:, :n], m[:, :n], l[:, :n]
            update = dot(jnp.concatenate([lh, lh, lm, lm, lh, ll], 0), jnp.concatenate([h, m, h, m, l, h], 0), 0, 0)
            start = 8 * (first + 4)
            work[start:, :] = work[start:, :] - update[start:]
        column = ahead
    return jnp.concatenate([right[p] for p in range(panels)], 0)


def solve_kernel(rank, *refs, scale):
    me_y, core_id, first, second = position()
    pieces, start, hls, w2 = refs[:8], refs[8], refs[9], refs[10]
    basis_out, core0, core1, core2, core3, param_out = refs[11:17]
    packed, gh, gm, gl, hl, last, work, core, qhl, iterate, sem = refs[17:]
    ends = [(w2, last) if d == 2 else (hls.at[d], hl.at[d]) for d in range(NY)]
    copies = [pltpu.make_async_copy(x, y, sem.at[d]) for d, (x, y) in enumerate(ends)]
    for copy in copies:
        copy.start()
    blocks, rows, t = pieces[0].shape
    for n, piece in enumerate(pieces):
        half, base = (core_id, first) if n < NX else (1 - core_id, second)
        at = pl.multiple_of(half * (t // 2) + around(base, NX - n % NX) * rows, rows)
        packed[:, pl.ds(at, rows), :] = piece[...]
    for n, (i, j) in enumerate(
        [(around(me_y, d), around(me_y, d + 1)) for d in range(NY)]
        + [tuple(around(me_y, d) for d in low_first(me_y, e, e + 2)) for e in range(2)]
        + [(around(me_y, d), around(me_y, d)) for d in range(NY)]
    ):
        block = packed[n] * scale
        for k, g in enumerate(split3(block)):
            (gh, gm, gl)[k][i, :, pl.ds(pl.multiple_of(j * t, t), t)] = g
        if n < 6:
            for k, g in enumerate(split3(block.T)):
                (gh, gm, gl)[k][j, :, pl.ds(pl.multiple_of(i * t, t), t)] = g

    iterate[...] = start[...].T
    n = iterate.shape[0]

    def step(_, carry):
        h, m, l = split3(iterate[...])
        by_h = dot(jnp.concatenate([h, m, l], 0), gh[...].reshape(NY * t, NY * t), 1, 0)
        by_m = dot(jnp.concatenate([h, m], 0), gm[...].reshape(NY * t, NY * t), 1, 0)
        by_l = dot(h, gl[...].reshape(NY * t, NY * t), 1, 0)
        image = by_h[:n] + ((by_h[n : 2 * n] + by_m[:n]) + (by_h[2 * n :] + by_m[n:] + by_l))
        h, m, l = split3(image)
        by_h = dot(jnp.concatenate([h, m, l], 0), h, 1, 1)
        small = by_h[n : 2 * n] + by_h[2 * n :]
        work[:, :n] = by_h[:n] + ((small + small.T) + dot(m, m, 1, 1))
        ih, im, il = split3(cholesky_inverse(work))
        by_h = dot(jnp.concatenate([ih, im, il], 0), h, 1, 0)
        by_m = dot(jnp.concatenate([ih, im], 0), m, 1, 0)
        iterate[...] = by_h[:n] + ((by_h[n : 2 * n] + by_m[:n]) + (by_h[2 * n :] + by_m[n:] + dot(ih, l, 1, 0)))
        return carry

    lax.fori_loop(0, ITERS, step, 0)
    q = iterate[...]
    slot = lax.broadcasted_iota(jnp.int32, q.shape, 0)
    q = jnp.where(slot < rank[0], q, 0.0)
    basis_out[...] = q.T
    qhl[0], qhl[1] = split2(q)
    total = None
    for d in range(NY):
        copies[d].wait()
        if d == 2:
            hl[2, 0], hl[2, 1] = split2(last[...])
        at = pl.ds(pl.multiple_of(around(me_y, d) * t, t), t)
        hs, ls = qhl[0, :, at], qhl[1, :, at]
        by_hi = dot(jnp.concatenate([hs, ls], 0), hl[d, 0], 1, 0)
        term = by_hi[:n] + (by_hi[n:] + dot(hs, hl[d, 1], 1, 0))
        total = term if total is None else total + term
    core[...] = total
    own = n // NY
    for k, out in enumerate((core0, core1, core2, core3)):
        out[...] = core[pl.ds(pl.multiple_of(around(me_y, k) * own, 8), own), :]
    h, l = split2(total)
    param = jnp.zeros((PARAMS, PARAMS), F32)
    for s in range(total.shape[1] // PARAMS):
        hs, ls = h[:, s * PARAMS : (s + 1) * PARAMS], l[:, s * PARAMS : (s + 1) * PARAMS]
        cross = dot(hs, ls, 0, 0)
        param = param + (dot(hs, hs, 0, 0) + (cross + cross.T) + dot(ls, ls, 0, 0))
    param_out[...] = param


def solve(rank, pieces, start_basis, hls, w2, scale):
    time_all, ranks = start_basis.shape
    blocks, _, t = pieces[0].shape
    width = w2.shape[1]
    struct = jax.ShapeDtypeStruct
    part = struct((ranks // NY, width), F32)
    vmem = pl.BlockSpec(memory_space=VMEM)
    smem = pl.BlockSpec(memory_space=SMEM)
    hbm = pl.BlockSpec(memory_space=HBM)

    def body(*refs):
        solve_kernel(*refs, scale=scale)

    return pl.pallas_call(
        body,
        out_shape=(struct((time_all, ranks), F32), part, part, part, part, struct((PARAMS, PARAMS), F32)),
        in_specs=[smem] + [vmem] * 9 + [hbm] * 2,
        out_specs=[vmem] * 6,
        scratch_shapes=[
            VMEM((blocks, t, t), F32),
            VMEM((NY, t, time_all), BF16),
            VMEM((NY, t, time_all), BF16),
            VMEM((NY, t, time_all), BF16),
            VMEM((NY, 2, t, width), BF16),
            VMEM((t, width), F32),
            VMEM((ranks, 2 * ranks), F32),
            VMEM((ranks, width), F32),
            VMEM((2, ranks, time_all), BF16),
            VMEM((ranks, time_all), F32),
            pltpu.SemaphoreType.DMA((NY,)),
        ],
        compiler_params=pltpu.CompilerParams(vmem_limit_bytes=28 * 2**20),
        cost_estimate=pl.CostEstimate(flops=8 * 10**9, bytes_accessed=9 * 2**20, transcendentals=0),
        name="solve",
    )(rank, *pieces, start_basis, hls, w2)


def join_kernel(p0, p1, p2, p3, out):
    me_y = lax.axis_index("tm")
    width = p0.shape[1]
    for k, piece in enumerate((p0, p1, p2, p3)):
        out[:, pl.ds(pl.multiple_of(around(me_y, NY - k) * width, 128), width)] = piece[...]


def join_columns(pieces):
    rows, width = pieces[0].shape
    return pl.pallas_call(
        join_kernel,
        out_shape=jax.ShapeDtypeStruct((rows, NY * width), F32),
        in_specs=[pl.BlockSpec(memory_space=VMEM)] * 4,
        out_specs=pl.BlockSpec(memory_space=VMEM),
        compiler_params=pltpu.CompilerParams(vmem_limit_bytes=4 * 2**20),
        name="join_columns",
    )(*pieces)


def scatter_sum(v, me, move):
    v = v.reshape(v.shape[0], NX, v.shape[1] // NX, v.shape[2])

    def slot(k):
        return lax.dynamic_index_in_dim(v, (me + k) % NX, 1, keepdims=False)

    got = [move(slot(k), k) for k in (1, 3, 2)]
    return slot(0) + got[0] + got[1] + got[2]


def exchange_sum(v, move):
    got = [move(v, k) for k in (1, 3, 2)]
    return v + got[0] + got[1] + got[2]


def gather(v, move):
    got = {k: move(v, k) for k in (1, 3, 2)}
    return [v, got[1], got[2], got[3]]


def local(slab, start_basis, time_rank):
    rest_count = lax.axis_size("rest")
    columns_local = slab.shape[1]
    columns_all = columns_local * rest_count
    width = columns_local // NY
    ranks = start_basis.shape[1]
    _, _, first_me, _ = position()

    def scatter(send, keep):
        return scatter_sum(keep + along_core(send), first_me, lambda w, k: along_xz(w, k, True))

    def exchange(u):
        return exchange_sum(u, lambda w, k: along_xz(w, k, False))

    next_cols, last_cols = slices(slab)
    w1, w3 = along_y(next_cols, 1), along_y(last_cols, 3)
    send0, keep0, hl0, across = gram_call(own_kernel, "own_gram", [slab], [], 0, columns_local, 1, width)
    w1, w3, across = lax.optimization_barrier((w1, w3, across))
    w2 = along_y(across, 2)
    send, keep, hls = gram_call(early_kernel, "early_gram", [w1, w3, send0, keep0], [hl0], 4, width, 1, width)
    early = scatter(send, keep)
    early, w2 = lax.optimization_barrier((early, w2))
    early = exchange(early)
    send, keep = gram_call(late_kernel, "late_gram", [w2], [hls], 3, width, 0, width)
    late = exchange(scatter(send, keep))
    v = jnp.concatenate([early, late])
    got = {k: along_y(v, k) for k in (1, 3, 2)}
    at = [v, got[3], got[2], got[1]]

    def term(d, n):
        return at[d % NY][n]

    v = jnp.stack(
        [term(d, 1) + term(d + 1, 2) + term(d + 2, 5) + term(d + 3, 6) for d in range(NY)]
        + [term(d, 4) + term(d + 2, 4) + term(d + 1, 3) + term(d + 3, 3) for d in range(2)]
        + [term(d, 0) for d in range(NY)]
    )
    pieces = gather(v, lambda u, k: along_xz(u, k, True))
    pieces = pieces + [along_core(piece) for piece in pieces]
    basis, *cores, param = solve(time_rank, pieces, start_basis, hls, w2, 1.0 / columns_all)

    param = param + along_core(param)
    param = exchange_sum(param, lambda u, k: along_xz(u, k, True))
    param = exchange_sum(param, lambda u, k: along_xz(u, k, False))
    param = exchange_sum(param, along_y)
    space_all = columns_local // PARAMS * rest_count
    param_gram = param / float(ranks * space_all)

    mine = {k: along_y(cores[k], k) for k in (1, 3, 2)}
    core = join_columns([cores[0], mine[1], mine[2], mine[3]])
    return (basis, core, param_gram)


def solution(mesh):
    in_specs = (P("tm", "rest"), P(), P())
    out_specs = (P(), P("tm", "rest"), P())
    return jax.shard_map(local, mesh=mesh, in_specs=in_specs, out_specs=out_specs, check_vma=False)
```

```python
import jax
import jax.numpy as jnp
from jax import lax
from jax.experimental import pallas as pl
from jax.experimental.pallas import tpu as pltpu
from jax.sharding import PartitionSpec as P

F32, BF16 = jnp.float32, jnp.bfloat16
PARAMS = 128
ITERS = 3
HELD = 56
COST = {"own_gram": 10**9, "early_gram": 10**9, "late_gram": 2 * 10**10}
NY, NX, NZ = 4, 4, 4
VMEM, SMEM, HBM = pltpu.VMEM, pltpu.SMEM, pltpu.HBM


def rest_index(x, z, c):
    return (x * NZ + z) * 2 + c


def along_y(v, k):
    return lax.ppermute(v, "tm", [(i, (i + k) % NY) for i in range(NY)])


def along_core(v):
    return lax.ppermute(v, "rest", [(i, i ^ 1) for i in range(2 * NX * NZ)])


def along_xz(v, k, first):
    perm = []
    for x in range(NX):
        for z in range(NZ):
            for c in range(2):
                if (c == 0) == first:
                    to = rest_index((x + k) % NX, z, c)
                else:
                    to = rest_index(x, (z + k) % NZ, c)
                perm.append((rest_index(x, z, c), to))
    return lax.ppermute(v, "rest", perm)


def position():
    me_y, rest = lax.axis_index("tm"), lax.axis_index("rest")
    core, z, x = lax.rem(rest, 2), lax.rem(lax.div(rest, 2), NZ), lax.div(rest, 2 * NZ)
    return me_y, core, jnp.where(core == 0, x, z), jnp.where(core == 0, z, x)


def around(i, k):
    return lax.rem(i + k, 4)


def low_first(me, i, j):
    swap = around(me, i) > around(me, j)
    return jnp.where(swap, j, i), jnp.where(swap, i, j)


def split2(v):
    hi = v.astype(BF16)
    return hi, (v - hi.astype(F32)).astype(BF16)


def split3(v):
    hi = v.astype(BF16)
    rest = v - hi.astype(F32)
    mid = rest.astype(BF16)
    return hi, mid, (rest - mid.astype(F32)).astype(BF16)


def dot(a, b, ca, cb):
    return lax.dot_general(a, b, (((ca,), (cb,)), ((), ())), preferred_element_type=F32)


def product(hl, i, j, core, out):
    h, l = hl.at[i], hl.at[j]
    total = dot(h[0], l[0], 1, 1) + (dot(h[1], l[0], 1, 1) + dot(h[0], l[1], 1, 1) + dot(h[1], l[1], 1, 1))
    half = total.shape[0] // 2
    out[0][...] = jnp.where(core == 0, total[half:], total[:half])
    out[1][...] = jnp.where(core == 0, total[:half], total[half:])


def own_kernel(slab, send, keep, hl_out, across, hl, sem):
    me_y, core, _, _ = position()
    h, l = split2(slab[...])
    hl[0, 0], hl[0, 1] = h, l
    width = hl_out.shape[2]
    mine = pl.ds(pl.multiple_of(me_y * width, 128), width)
    theirs = pl.ds(pl.multiple_of(around(me_y, 2) * width, 128), width)
    outs = [
        pltpu.make_async_copy(hl.at[0, :, :, mine], hl_out, sem.at[0]),
        pltpu.make_async_copy(slab.at[:, theirs], across, sem.at[1]),
    ]
    for out in outs:
        out.start()
    product(hl, 0, 0, core, (send, keep))
    for out in outs:
        out.wait()


def slices_kernel(slab, ahead, behind, held, sem):
    me_y = lax.axis_index("tm")
    width = ahead.shape[1]
    rows = held.shape[2]
    ins, outs = [], []
    for n, (k, out) in enumerate(((1, ahead), (3, behind))):
        at = pl.ds(pl.multiple_of(around(me_y, k) * width, 128), width)
        for r in range(held.shape[1]):
            part = pl.ds(r * rows, rows)
            ins.append(pltpu.make_async_copy(slab.at[part, at], held.at[n, r], sem.at[0, n, r]))
            outs.append(pltpu.make_async_copy(held.at[n, r], out.at[part, :], sem.at[1, n, r]))
    for copy in ins:
        copy.start()
    for copy, out in zip(ins, outs):
        copy.wait()
        out.start()
    for out in outs:
        out.wait()


def slices(slab):
    out = jax.ShapeDtypeStruct((slab.shape[0], slab.shape[1] // NY), F32)
    hbm = pl.BlockSpec(memory_space=HBM)
    parts = 4
    return pl.pallas_call(
        slices_kernel,
        out_shape=[out, out],
        in_specs=[hbm],
        out_specs=[hbm, hbm],
        scratch_shapes=[
            VMEM((2, parts, out.shape[0] // parts, out.shape[1]), F32),
            pltpu.SemaphoreType.DMA((2, 2, parts)),
        ],
        compiler_params=pltpu.CompilerParams(vmem_limit_bytes=56 * 2**20),
        name="slices",
    )(slab)


def early_kernel(w1, w3, send0, keep0, hl0, send, keep, hls, hl, sem):
    me_y, core, _, _ = position()
    copy = pltpu.make_async_copy(hl0, hl.at[0], sem.at[0])
    copy.start()
    for w, d in ((w1, 3), (w3, 1)):
        h, l = split2(w[...])
        hl[d, 0], hl[d, 1] = h, l
    outs = [pltpu.make_async_copy(hl.at[d], hls.at[d], sem.at[d]) for d in (1, 3, 0)]
    for out in outs[:2]:
        out.start()
    send[0], keep[0] = send0[...], keep0[...]
    copy.wait()
    outs[2].start()
    for n, (i, j) in enumerate(((0, 1), (3, 0), low_first(me_y, 3, 1))):
        product(hl, i, j, core, (send.at[n + 1], keep.at[n + 1]))
    for out in outs:
        out.wait()


def late_kernel(w2, hls, send, keep, hl, sem):
    me_y, core, _, _ = position()
    copies = [pltpu.make_async_copy(hls.at[d], hl.at[d], sem.at[d]) for d in (0, 3, 1)]
    for copy in copies:
        copy.start()
    h, l = split2(w2[...])
    hl[2, 0], hl[2, 1] = h, l
    for n, (i, j) in enumerate((low_first(me_y, 0, 2), (2, 3), (1, 2))):
        copies[n].wait()
        product(hl, i, j, core, (send.at[n], keep.at[n]))


def gram_call(kernel, name, vmem_args, hbm_args, blocks, wide, halves, cols):
    rows = 256
    struct = jax.ShapeDtypeStruct
    vmem, hbm = pl.BlockSpec(memory_space=VMEM), pl.BlockSpec(memory_space=HBM)
    half = struct((blocks, rows // 2, rows) if blocks else (rows // 2, rows), F32)
    slots = NY if hbm_args else 1
    return pl.pallas_call(
        kernel,
        out_shape=[half, half] + [struct((2, rows, cols) if blocks == 0 else (HELD, 2, rows, cols), BF16)] * halves + [struct((rows, cols), F32)] * (1 - slots // NY),
        in_specs=[vmem] * len(vmem_args) + [hbm] * len(hbm_args),
        out_specs=[vmem] * 2 + [hbm] * (halves + 1 - slots // NY),
        scratch_shapes=[VMEM((slots, 2, rows, wide), BF16), pltpu.SemaphoreType.DMA((NY,))],
        compiler_params=pltpu.CompilerParams(vmem_limit_bytes=16 * 2**20),
        cost_estimate=pl.CostEstimate(flops=COST.get(name, 10**9), bytes_accessed=1000, transcendentals=0),
        name=name,
    )(*vmem_args, *hbm_args)


def chain(pairs, ca, cb):
    total = None
    for a, b in pairs:
        term = dot(a, b, ca, cb)
        total = term if total is None else total + term
    return total


def row_of(v, k):
    return jnp.broadcast_to(v[k : k + 1, :], v.shape)


def cholesky_inverse(work):
    n = work.shape[0]
    panels = n // 8
    r = lax.broadcasted_iota(jnp.int32, (n, n), 0)
    c = lax.broadcasted_iota(jnp.int32, (n, n), 1)
    work[:, n:] = (r == c).astype(F32)
    row = lax.broadcasted_iota(jnp.int32, (8, n), 0)
    left, right = {}, {}

    def load(t):
        left[t], right[t] = work[8 * t : 8 * t + 8, :n], work[8 * t : 8 * t + 8, n:]

    def columns(t, p):
        return [jnp.broadcast_to(left[t][:, 8 * p + j : 8 * p + j + 1], (8, n)) for j in range(8)]

    for t in range(2):
        load(t)
    column = columns(0, 0)
    for p in range(panels):
        first = p - p % 2
        if p == first:
            for t in range(first + 2, min(first + 4, panels)):
                load(t)
        below = range(p + 1, min(first + 4, panels))
        entries = {t: columns(t, p) for t in below}
        ahead = columns(p + 1, p + 1) if below else None
        scale = jnp.zeros((8, n), F32)
        for k in range(8):
            pivot = row_of(column[k], k)
            inverse = 1.0 / pivot
            scale = jnp.where(row == k, lax.rsqrt(pivot), scale)
            factor = jnp.where(row > k, column[k] * inverse, 0.0)
            across = [row_of(column[j], k) for j in range(k + 1, 8)]
            for j in range(k + 1, 8):
                column[j] = column[j] - factor * across[j - k - 1]
            left_k, right_k = row_of(left[p], k), row_of(right[p], k)
            left[p], right[p] = left[p] - factor * left_k, right[p] - factor * right_k
            for t in below:
                factor = entries[t][k] * inverse
                if t == p + 1:
                    ahead = [ahead[j] - factor * row_of(entries[t][k], j) for j in range(8)]
                for j in range(k + 1, 8):
                    entries[t][j] = entries[t][j] - factor * across[j - k - 1]
                left[t], right[t] = left[t] - factor * left_k, right[t] - factor * right_k
        left[p], right[p] = left[p] * scale, right[p] * scale
        if p > first and first + 4 < panels:
            h, m, l = split3(jnp.concatenate([jnp.concatenate([left[t], right[t]], 1) for t in (first, p)], 0))
            lh, lm, ll = h[:, :n], m[:, :n], l[:, :n]
            start = 8 * (first + 4)
            a = jnp.concatenate([lh, lh, lm, lm, lh, ll], 0)
            b = jnp.concatenate([h, m, h, m, l, h], 0)
            update = dot(a.T[start:], b, 1, 0)
            work[start:, :] = work[start:, :] - update
        column = ahead
    return jnp.concatenate([right[p] for p in range(panels)], 0)


def solve_kernel(rank, *refs, scale):
    me_y, core_id, first, second = position()
    pieces, start, hls, w2 = refs[:8], refs[8], refs[9], refs[10]
    basis_out, core0, core1, core2, core3, param_out = refs[11:17]
    packed, gh, gm, gl, hl, last, work, core, qhl, iterate, sem = refs[17:]
    ends = [(w2, last) if d == 2 else (hls.at[d], hl.at[d]) for d in range(NY)]
    copies = [pltpu.make_async_copy(x, y, sem.at[d]) for d, (x, y) in enumerate(ends)]
    for copy in copies:
        copy.start()
    blocks, rows, t = pieces[0].shape
    for n, piece in enumerate(pieces):
        half, base = (core_id, first) if n < NX else (1 - core_id, second)
        at = pl.multiple_of(half * (t // 2) + around(base, NX - n % NX) * rows, rows)
        packed[:, pl.ds(at, rows), :] = piece[...]
    for n, (i, j) in enumerate(
        [(around(me_y, d), around(me_y, d + 1)) for d in range(NY)]
        + [tuple(around(me_y, d) for d in low_first(me_y, e, e + 2)) for e in range(2)]
        + [(around(me_y, d), around(me_y, d)) for d in range(NY)]
    ):
        block = packed[n] * scale
        for k, g in enumerate(split3(block)):
            (gh, gm, gl)[k][i, :, pl.ds(pl.multiple_of(j * t, t), t)] = g
        if n < 6:
            for k, g in enumerate(split3(block.T)):
                (gh, gm, gl)[k][j, :, pl.ds(pl.multiple_of(i * t, t), t)] = g

    iterate[...] = start[...].T
    n = iterate.shape[0]

    def step(_, carry):
        h, m, l = split3(iterate[...])
        wide = [g[...].reshape(NY * t, NY * t) for g in (gh, gm, gl)]
        image = dot(h, wide[0], 1, 0) + (
            (dot(m, wide[0], 1, 0) + dot(h, wide[1], 1, 0))
            + (dot(l, wide[0], 1, 0) + dot(m, wide[1], 1, 0) + dot(h, wide[2], 1, 0))
        )
        h, m, l = split3(image)
        small = dot(l, h, 1, 1) + dot(m, h, 1, 1)
        work[:, :n] = dot(h, h, 1, 1) + ((small + small.T) + dot(m, m, 1, 1))
        ih, im, il = split3(cholesky_inverse(work))
        by_h = dot(jnp.concatenate([ih, im, il], 0), h, 1, 0)
        by_m = dot(jnp.concatenate([ih, im], 0), m, 1, 0)
        iterate[...] = by_h[:n] + ((by_h[n : 2 * n] + by_m[:n]) + (by_h[2 * n :] + by_m[n:] + dot(ih, l, 1, 0)))
        return carry

    lax.fori_loop(0, ITERS, step, 0)
    q = iterate[...]
    slot = lax.broadcasted_iota(jnp.int32, q.shape, 0)
    q = jnp.where(slot < rank[0], q, 0.0)
    basis_out[...] = q.T
    qhl[0], qhl[1] = split2(q)
    total = None
    for d in range(NY):
        copies[d].wait()
        if d == 2:
            hl[2, 0], hl[2, 1] = split2(last[...])
        at = pl.ds(pl.multiple_of(around(me_y, d) * t, t), t)
        hs, ls = qhl[0, :, at], qhl[1, :, at]
        term = dot(hs, hl[d, 0], 1, 0) + (dot(ls, hl[d, 0], 1, 0) + dot(hs, hl[d, 1], 1, 0))
        total = term if total is None else total + term
    core[...] = total
    own = n // NY
    for k, out in enumerate((core0, core1, core2, core3)):
        out[...] = core[pl.ds(pl.multiple_of(around(me_y, k) * own, 8), own), :]
    h, l = split2(total)
    param = jnp.zeros((PARAMS, PARAMS), F32)
    for s in range(total.shape[1] // PARAMS):
        hs, ls = h[:, s * PARAMS : (s + 1) * PARAMS], l[:, s * PARAMS : (s + 1) * PARAMS]
        cross = dot(hs, ls, 0, 0)
        param = param + (dot(hs, hs, 0, 0) + (cross + cross.T) + dot(ls, ls, 0, 0))
    param_out[...] = param


def solve(rank, pieces, start_basis, hls, w2, scale):
    time_all, ranks = start_basis.shape
    blocks, _, t = pieces[0].shape
    width = w2.shape[1]
    struct = jax.ShapeDtypeStruct
    part = struct((ranks // NY, width), F32)
    vmem = pl.BlockSpec(memory_space=VMEM)
    smem = pl.BlockSpec(memory_space=SMEM)
    hbm = pl.BlockSpec(memory_space=HBM)

    def body(*refs):
        solve_kernel(*refs, scale=scale)

    return pl.pallas_call(
        body,
        out_shape=(struct((time_all, ranks), F32), part, part, part, part, struct((PARAMS, PARAMS), F32)),
        in_specs=[smem] + [vmem] * 9 + [hbm] * 2,
        out_specs=[vmem] * 6,
        scratch_shapes=[
            VMEM((blocks, t, t), F32),
            VMEM((NY, t, time_all), BF16),
            VMEM((NY, t, time_all), BF16),
            VMEM((NY, t, time_all), BF16),
            VMEM((NY, 2, t, width), BF16),
            VMEM((t, width), F32),
            VMEM((ranks, 2 * ranks), F32),
            VMEM((ranks, width), F32),
            VMEM((2, ranks, time_all), BF16),
            VMEM((ranks, time_all), F32),
            pltpu.SemaphoreType.DMA((NY,)),
        ],
        compiler_params=pltpu.CompilerParams(vmem_limit_bytes=28 * 2**20),
        cost_estimate=pl.CostEstimate(flops=8 * 10**9, bytes_accessed=9 * 2**20, transcendentals=0),
        name="solve",
    )(rank, *pieces, start_basis, hls, w2)


def join_kernel(p0, p1, p2, p3, out):
    me_y = lax.axis_index("tm")
    width = p0.shape[1]
    for k, piece in enumerate((p0, p1, p2, p3)):
        out[:, pl.ds(pl.multiple_of(around(me_y, NY - k) * width, 128), width)] = piece[...]


def join_columns(pieces):
    rows, width = pieces[0].shape
    return pl.pallas_call(
        join_kernel,
        out_shape=jax.ShapeDtypeStruct((rows, NY * width), F32),
        in_specs=[pl.BlockSpec(memory_space=VMEM)] * 4,
        out_specs=pl.BlockSpec(memory_space=VMEM),
        compiler_params=pltpu.CompilerParams(vmem_limit_bytes=4 * 2**20),
        name="join_columns",
    )(*pieces)


def scatter_sum(v, me, move):
    v = v.reshape(v.shape[0], NX, v.shape[1] // NX, v.shape[2])

    def slot(k):
        return lax.dynamic_index_in_dim(v, (me + k) % NX, 1, keepdims=False)

    got = [move(slot(k), k) for k in (1, 3, 2)]
    return slot(0) + got[0] + got[1] + got[2]


def exchange_sum(v, move):
    got = [move(v, k) for k in (1, 3, 2)]
    return v + got[0] + got[1] + got[2]


def gather(v, move):
    got = {k: move(v, k) for k in (1, 3, 2)}
    return [v, got[1], got[2], got[3]]


def local(slab, start_basis, time_rank):
    rest_count = lax.axis_size("rest")
    columns_local = slab.shape[1]
    columns_all = columns_local * rest_count
    width = columns_local // NY
    ranks = start_basis.shape[1]
    _, _, first_me, _ = position()

    def scatter(send, keep):
        return scatter_sum(keep + along_core(send), first_me, lambda w, k: along_xz(w, k, True))

    def exchange(u):
        return exchange_sum(u, lambda w, k: along_xz(w, k, False))

    next_cols, last_cols = slices(slab)
    w1, w3 = along_y(next_cols, 1), along_y(last_cols, 3)
    send0, keep0, hl0, across = gram_call(own_kernel, "own_gram", [slab], [], 0, columns_local, 1, width)
    w1, w3, across = lax.optimization_barrier((w1, w3, across))
    w2 = along_y(across, 2)
    send, keep, hls = gram_call(early_kernel, "early_gram", [w1, w3, send0, keep0], [hl0], 4, width, 1, width)
    early = scatter(send, keep)
    early, w2 = lax.optimization_barrier((early, w2))
    early = exchange(early)
    send, keep = gram_call(late_kernel, "late_gram", [w2], [hls], 3, width, 0, width)
    late = exchange(scatter(send, keep))
    v = jnp.concatenate([early, late])
    got = {k: along_y(v, k) for k in (1, 3, 2)}
    at = [v, got[3], got[2], got[1]]

    def term(d, n):
        return at[d % NY][n]

    v = jnp.stack(
        [term(d, 1) + term(d + 1, 2) + term(d + 2, 5) + term(d + 3, 6) for d in range(NY)]
        + [term(d, 4) + term(d + 2, 4) + term(d + 1, 3) + term(d + 3, 3) for d in range(2)]
        + [term(d, 0) for d in range(NY)]
    )
    pieces = gather(v, lambda u, k: along_xz(u, k, True))
    pieces = pieces + [along_core(piece) for piece in pieces]
    basis, *cores, param = solve(time_rank, pieces, start_basis, hls, w2, 1.0 / columns_all)

    param = param + along_core(param)
    param = exchange_sum(param, lambda u, k: along_xz(u, k, True))
    param = exchange_sum(param, lambda u, k: along_xz(u, k, False))
    param = exchange_sum(param, along_y)
    space_all = columns_local // PARAMS * rest_count
    param_gram = param / float(ranks * space_all)

    mine = {k: along_y(cores[k], k) for k in (1, 3, 2)}
    core = join_columns([cores[0], mine[1], mine[2], mine[3]])
    return (basis, core, param_gram)


def solution(mesh):
    in_specs = (P("tm", "rest"), P(), P())
    out_specs = (P(), P("tm", "rest"), P())
    return jax.shard_map(local, mesh=mesh, in_specs=in_specs, out_specs=out_specs, check_vma=False)
```

```python
import jax
import jax.numpy as jnp
from jax import lax
from jax.experimental import pallas as pl
from jax.experimental.pallas import tpu as pltpu
from jax.sharding import PartitionSpec as P

F32, BF16 = jnp.float32, jnp.bfloat16
PARAMS = 128
ITERS = 3
HELD = 56
COST = {"own_gram": 10**9, "early_gram": 10**9, "late_gram": 2 * 10**10}
NY, NX, NZ = 4, 4, 4
VMEM, SMEM, HBM = pltpu.VMEM, pltpu.SMEM, pltpu.HBM


def rest_index(x, z, c):
    return (x * NZ + z) * 2 + c


def along_y(v, k):
    return lax.ppermute(v, "tm", [(i, (i + k) % NY) for i in range(NY)])


def along_core(v):
    return lax.ppermute(v, "rest", [(i, i ^ 1) for i in range(2 * NX * NZ)])


def along_xz(v, k, first):
    perm = []
    for x in range(NX):
        for z in range(NZ):
            for c in range(2):
                if (c == 0) == first:
                    to = rest_index((x + k) % NX, z, c)
                else:
                    to = rest_index(x, (z + k) % NZ, c)
                perm.append((rest_index(x, z, c), to))
    return lax.ppermute(v, "rest", perm)


def position():
    me_y, rest = lax.axis_index("tm"), lax.axis_index("rest")
    core, z, x = lax.rem(rest, 2), lax.rem(lax.div(rest, 2), NZ), lax.div(rest, 2 * NZ)
    return me_y, core, jnp.where(core == 0, x, z), jnp.where(core == 0, z, x)


def around(i, k):
    return lax.rem(i + k, 4)


def low_first(me, i, j):
    swap = around(me, i) > around(me, j)
    return jnp.where(swap, j, i), jnp.where(swap, i, j)


def split2(v):
    hi = v.astype(BF16)
    return hi, (v - hi.astype(F32)).astype(BF16)


def split3(v):
    hi = v.astype(BF16)
    rest = v - hi.astype(F32)
    mid = rest.astype(BF16)
    return hi, mid, (rest - mid.astype(F32)).astype(BF16)


def dot(a, b, ca, cb):
    return lax.dot_general(a, b, (((ca,), (cb,)), ((), ())), preferred_element_type=F32)


def product(hl, i, j, core, out):
    h, l = hl.at[i], hl.at[j]
    total = dot(h[0], l[0], 1, 1) + (dot(h[1], l[0], 1, 1) + dot(h[0], l[1], 1, 1) + dot(h[1], l[1], 1, 1))
    half = total.shape[0] // 2
    out[0][...] = jnp.where(core == 0, total[half:], total[:half])
    out[1][...] = jnp.where(core == 0, total[:half], total[half:])


def own_kernel(slab, send, keep, hl_out, across, hl, sem):
    me_y, core, _, _ = position()
    h, l = split2(slab[...])
    hl[0, 0], hl[0, 1] = h, l
    width = hl_out.shape[2]
    mine = pl.ds(pl.multiple_of(me_y * width, 128), width)
    theirs = pl.ds(pl.multiple_of(around(me_y, 2) * width, 128), width)
    outs = [
        pltpu.make_async_copy(hl.at[0, :, :, mine], hl_out, sem.at[0]),
        pltpu.make_async_copy(slab.at[:, theirs], across, sem.at[1]),
    ]
    for out in outs:
        out.start()
    product(hl, 0, 0, core, (send, keep))
    for out in outs:
        out.wait()


def slices_kernel(slab, ahead, behind, held, sem):
    me_y = lax.axis_index("tm")
    width = ahead.shape[1]
    rows = held.shape[2]
    ins, outs = [], []
    for n, (k, out) in enumerate(((1, ahead), (3, behind))):
        at = pl.ds(pl.multiple_of(around(me_y, k) * width, 128), width)
        for r in range(held.shape[1]):
            part = pl.ds(r * rows, rows)
            ins.append(pltpu.make_async_copy(slab.at[part, at], held.at[n, r], sem.at[0, n, r]))
            outs.append(pltpu.make_async_copy(held.at[n, r], out.at[part, :], sem.at[1, n, r]))
    for copy in ins:
        copy.start()
    for copy, out in zip(ins, outs):
        copy.wait()
        out.start()
    for out in outs:
        out.wait()


def slices(slab):
    out = jax.ShapeDtypeStruct((slab.shape[0], slab.shape[1] // NY), F32)
    hbm = pl.BlockSpec(memory_space=HBM)
    parts = 4
    return pl.pallas_call(
        slices_kernel,
        out_shape=[out, out],
        in_specs=[hbm],
        out_specs=[hbm, hbm],
        scratch_shapes=[
            VMEM((2, parts, out.shape[0] // parts, out.shape[1]), F32),
            pltpu.SemaphoreType.DMA((2, 2, parts)),
        ],
        compiler_params=pltpu.CompilerParams(vmem_limit_bytes=56 * 2**20),
        name="slices",
    )(slab)


def early_kernel(w1, w3, send0, keep0, hl0, send, keep, hls, hl, sem):
    me_y, core, _, _ = position()
    copy = pltpu.make_async_copy(hl0, hl.at[0], sem.at[0])
    copy.start()
    for w, d in ((w1, 3), (w3, 1)):
        h, l = split2(w[...])
        hl[d, 0], hl[d, 1] = h, l
    outs = [pltpu.make_async_copy(hl.at[d], hls.at[d], sem.at[d]) for d in (1, 3, 0)]
    for out in outs[:2]:
        out.start()
    send[0], keep[0] = send0[...], keep0[...]
    copy.wait()
    outs[2].start()
    for n, (i, j) in enumerate(((0, 1), (3, 0), low_first(me_y, 3, 1))):
        product(hl, i, j, core, (send.at[n + 1], keep.at[n + 1]))
    for out in outs:
        out.wait()


def late_kernel(w2, hls, send, keep, hl, sem):
    me_y, core, _, _ = position()
    copies = [pltpu.make_async_copy(hls.at[d], hl.at[d], sem.at[d]) for d in (0, 3, 1)]
    for copy in copies:
        copy.start()
    h, l = split2(w2[...])
    hl[2, 0], hl[2, 1] = h, l
    for n, (i, j) in enumerate((low_first(me_y, 0, 2), (2, 3), (1, 2))):
        copies[n].wait()
        product(hl, i, j, core, (send.at[n], keep.at[n]))


def gram_call(kernel, name, vmem_args, hbm_args, blocks, wide, halves, cols):
    rows = 256
    struct = jax.ShapeDtypeStruct
    vmem, hbm = pl.BlockSpec(memory_space=VMEM), pl.BlockSpec(memory_space=HBM)
    half = struct((blocks, rows // 2, rows) if blocks else (rows // 2, rows), F32)
    slots = NY if hbm_args else 1
    return pl.pallas_call(
        kernel,
        out_shape=[half, half] + [struct((2, rows, cols) if blocks == 0 else (HELD, 2, rows, cols), BF16)] * halves + [struct((rows, cols), F32)] * (1 - slots // NY),
        in_specs=[vmem] * len(vmem_args) + [hbm] * len(hbm_args),
        out_specs=[vmem] * 2 + [hbm] * (halves + 1 - slots // NY),
        scratch_shapes=[VMEM((slots, 2, rows, wide), BF16), pltpu.SemaphoreType.DMA((NY,))],
        compiler_params=pltpu.CompilerParams(vmem_limit_bytes=16 * 2**20),
        cost_estimate=pl.CostEstimate(flops=COST.get(name, 10**9), bytes_accessed=1000, transcendentals=0),
        name=name,
    )(*vmem_args, *hbm_args)


def chain(pairs, ca, cb):
    total = None
    for a, b in pairs:
        term = dot(a, b, ca, cb)
        total = term if total is None else total + term
    return total


def row_of(v, k):
    return jnp.broadcast_to(v[k : k + 1, :], v.shape)


def cholesky_inverse(work):
    n = work.shape[0]
    panels = n // 8
    r = lax.broadcasted_iota(jnp.int32, (n, n), 0)
    c = lax.broadcasted_iota(jnp.int32, (n, n), 1)
    work[:, n:] = (r == c).astype(F32)
    row = lax.broadcasted_iota(jnp.int32, (8, n), 0)
    left, right = {}, {}

    def load(t):
        left[t], right[t] = work[8 * t : 8 * t + 8, :n], work[8 * t : 8 * t + 8, n:]

    def columns(t, p):
        return [jnp.broadcast_to(left[t][:, 8 * p + j : 8 * p + j + 1], (8, n)) for j in range(8)]

    for t in range(2):
        load(t)
    column = columns(0, 0)
    for p in range(panels):
        first = p - p % 2
        if p == first:
            for t in range(first + 2, min(first + 4, panels)):
                load(t)
        below = range(p + 1, min(first + 4, panels))
        entries = {t: columns(t, p) for t in below}
        ahead = columns(p + 1, p + 1) if below else None
        scale = jnp.zeros((8, n), F32)
        for k in range(8):
            pivot = row_of(column[k], k)
            inverse = 1.0 / pivot
            scale = jnp.where(row == k, lax.rsqrt(pivot), scale)
            factor = jnp.where(row > k, column[k] * inverse, 0.0)
            across = [row_of(column[j], k) for j in range(k + 1, 8)]
            for j in range(k + 1, 8):
                column[j] = column[j] - factor * across[j - k - 1]
            left_k, right_k = row_of(left[p], k), row_of(right[p], k)
            left[p], right[p] = left[p] - factor * left_k, right[p] - factor * right_k
            for t in below:
                factor = entries[t][k] * inverse
                if t == p + 1:
                    ahead = [ahead[j] - factor * row_of(entries[t][k], j) for j in range(8)]
                for j in range(k + 1, 8):
                    entries[t][j] = entries[t][j] - factor * across[j - k - 1]
                left[t], right[t] = left[t] - factor * left_k, right[t] - factor * right_k
        left[p], right[p] = left[p] * scale, right[p] * scale
        if p > first and first + 4 < panels:
            h, m, l = split3(jnp.concatenate([jnp.concatenate([left[t], right[t]], 1) for t in (first, p)], 0))
            lh, lm, ll = h[:, :n], m[:, :n], l[:, :n]
            start = 8 * (first + 4)
            a = jnp.concatenate([lh, lh, lm, lm, lh, ll], 0)
            b = jnp.concatenate([h, m, h, m, l, h], 0)
            update = dot(a.T[start:], b, 1, 0)
            work[start:, :] = work[start:, :] - update
        column = ahead
    return jnp.concatenate([right[p] for p in range(panels)], 0)


def swap_halves(v):
    half = v.shape[1] // 2
    return jnp.concatenate([v[:, half:], v[:, :half]], 1)


def places(shape):
    return lax.broadcasted_iota(jnp.int32, shape, 0), lax.broadcasted_iota(jnp.int32, shape, 1)


def pack_symmetric(v):
    n = v.shape[0]
    row, col = places((n // 2, n))
    body = jnp.where(col >= row, v[: n // 2], swap_halves(v[n // 2 :]))
    diagonal = jnp.sum(jnp.where(col == row + n // 2, v[n // 2 :], 0.0), 0, keepdims=True)
    return jnp.concatenate([body, jnp.broadcast_to(diagonal, (8, n))], 0)


def unpack_kernel(p0, p1, p2, p3, out, *, scale):
    v = (p0[...] + p1[...] + p2[...] + p3[...]) * scale
    n = v.shape[1]
    body, diagonal = v[: n // 2], v[n // 2 : n // 2 + 1]
    row, col = places((n // 2, n))
    upper = jnp.where(col >= row, body, 0.0)
    lower = jnp.where((col >= n // 2) & (col < row + n // 2), swap_halves(body), 0.0)
    lower = jnp.where(col == row + n // 2, jnp.broadcast_to(diagonal, lower.shape), lower)
    once = jnp.concatenate([upper, lower], 0)
    row, col = places((n, n))
    out[...] = once + jnp.where(row == col, 0.0, once.T)


def unpack_sum(pieces, scale):
    n = pieces[0].shape[1]

    def body(*refs):
        unpack_kernel(*refs, scale=scale)

    return pl.pallas_call(
        body,
        out_shape=jax.ShapeDtypeStruct((n, n), F32),
        in_specs=[pl.BlockSpec(memory_space=VMEM)] * 4,
        out_specs=pl.BlockSpec(memory_space=VMEM),
        compiler_params=pltpu.CompilerParams(vmem_limit_bytes=4 * 2**20),
        name="unpack_sum",
    )(*pieces)


def solve_kernel(rank, *refs, scale):
    me_y, core_id, first, second = position()
    pieces, start, hls, w2 = refs[:8], refs[8], refs[9], refs[10]
    basis_out, core0, core1, core2, core3, param_out = refs[11:17]
    packed, gh, gm, gl, hl, last, work, core, qhl, iterate, sem = refs[17:]
    ends = [(w2, last) if d == 2 else (hls.at[d], hl.at[d]) for d in range(NY)]
    copies = [pltpu.make_async_copy(x, y, sem.at[d]) for d, (x, y) in enumerate(ends)]
    for copy in copies:
        copy.start()
    blocks, rows, t = pieces[0].shape
    for n, piece in enumerate(pieces):
        half, base = (core_id, first) if n < NX else (1 - core_id, second)
        at = pl.multiple_of(half * (t // 2) + around(base, NX - n % NX) * rows, rows)
        packed[:, pl.ds(at, rows), :] = piece[...]
    for n, (i, j) in enumerate(
        [(around(me_y, d), around(me_y, d + 1)) for d in range(NY)]
        + [tuple(around(me_y, d) for d in low_first(me_y, e, e + 2)) for e in range(2)]
        + [(around(me_y, d), around(me_y, d)) for d in range(NY)]
    ):
        block = packed[n] * scale
        for k, g in enumerate(split3(block)):
            (gh, gm, gl)[k][i, :, pl.ds(pl.multiple_of(j * t, t), t)] = g
        if n < 6:
            for k, g in enumerate(split3(block.T)):
                (gh, gm, gl)[k][j, :, pl.ds(pl.multiple_of(i * t, t), t)] = g

    iterate[...] = start[...].T
    n = iterate.shape[0]

    def step(_, carry):
        h, m, l = split3(iterate[...])
        wide = [g[...].reshape(NY * t, NY * t) for g in (gh, gm, gl)]
        image = dot(h, wide[0], 1, 0) + (
            (dot(m, wide[0], 1, 0) + dot(h, wide[1], 1, 0))
            + (dot(l, wide[0], 1, 0) + dot(m, wide[1], 1, 0) + dot(h, wide[2], 1, 0))
        )
        h, m, l = split3(image)
        small = dot(l, h, 1, 1) + dot(m, h, 1, 1)
        work[:, :n] = dot(h, h, 1, 1) + ((small + small.T) + dot(m, m, 1, 1))
        ih, im, il = split3(cholesky_inverse(work))
        by_h = dot(jnp.concatenate([ih, im, il], 0), h, 1, 0)
        by_m = dot(jnp.concatenate([ih, im], 0), m, 1, 0)
        iterate[...] = by_h[:n] + ((by_h[n : 2 * n] + by_m[:n]) + (by_h[2 * n :] + by_m[n:] + dot(ih, l, 1, 0)))
        return carry

    lax.fori_loop(0, ITERS, step, 0)
    q = iterate[...]
    slot = lax.broadcasted_iota(jnp.int32, q.shape, 0)
    q = jnp.where(slot < rank[0], q, 0.0)
    basis_out[...] = q.T
    qhl[0], qhl[1] = split2(q)
    total = None
    for d in range(NY):
        copies[d].wait()
        if d == 2:
            hl[2, 0], hl[2, 1] = split2(last[...])
        at = pl.ds(pl.multiple_of(around(me_y, d) * t, t), t)
        hs, ls = qhl[0, :, at], qhl[1, :, at]
        term = dot(hs, hl[d, 0], 1, 0) + (dot(ls, hl[d, 0], 1, 0) + dot(hs, hl[d, 1], 1, 0))
        total = term if total is None else total + term
    core[...] = total
    own = n // NY
    for k, out in enumerate((core0, core1, core2, core3)):
        out[...] = core[pl.ds(pl.multiple_of(around(me_y, k) * own, 8), own), :]
    h, l = split2(total)
    param = jnp.zeros((PARAMS, PARAMS), F32)
    for s in range(total.shape[1] // PARAMS):
        hs, ls = h[:, s * PARAMS : (s + 1) * PARAMS], l[:, s * PARAMS : (s + 1) * PARAMS]
        cross = dot(hs, ls, 0, 0)
        param = param + (dot(hs, hs, 0, 0) + (cross + cross.T) + dot(ls, ls, 0, 0))
    param_out[...] = pack_symmetric(param)


def solve(rank, pieces, start_basis, hls, w2, scale):
    time_all, ranks = start_basis.shape
    blocks, _, t = pieces[0].shape
    width = w2.shape[1]
    struct = jax.ShapeDtypeStruct
    part = struct((ranks // NY, width), F32)
    vmem = pl.BlockSpec(memory_space=VMEM)
    smem = pl.BlockSpec(memory_space=SMEM)
    hbm = pl.BlockSpec(memory_space=HBM)

    def body(*refs):
        solve_kernel(*refs, scale=scale)

    return pl.pallas_call(
        body,
        out_shape=(struct((time_all, ranks), F32), part, part, part, part, struct((PARAMS // 2 + 8, PARAMS), F32)),
        in_specs=[smem] + [vmem] * 9 + [hbm] * 2,
        out_specs=[vmem] * 6,
        scratch_shapes=[
            VMEM((blocks, t, t), F32),
            VMEM((NY, t, time_all), BF16),
            VMEM((NY, t, time_all), BF16),
            VMEM((NY, t, time_all), BF16),
            VMEM((NY, 2, t, width), BF16),
            VMEM((t, width), F32),
            VMEM((ranks, 2 * ranks), F32),
            VMEM((ranks, width), F32),
            VMEM((2, ranks, time_all), BF16),
            VMEM((ranks, time_all), F32),
            pltpu.SemaphoreType.DMA((NY,)),
        ],
        compiler_params=pltpu.CompilerParams(vmem_limit_bytes=28 * 2**20),
        cost_estimate=pl.CostEstimate(flops=8 * 10**9, bytes_accessed=9 * 2**20, transcendentals=0),
        name="solve",
    )(rank, *pieces, start_basis, hls, w2)


def join_kernel(p0, p1, p2, p3, out):
    me_y = lax.axis_index("tm")
    width = p0.shape[1]
    for k, piece in enumerate((p0, p1, p2, p3)):
        out[:, pl.ds(pl.multiple_of(around(me_y, NY - k) * width, 128), width)] = piece[...]


def join_columns(pieces):
    rows, width = pieces[0].shape
    return pl.pallas_call(
        join_kernel,
        out_shape=jax.ShapeDtypeStruct((rows, NY * width), F32),
        in_specs=[pl.BlockSpec(memory_space=VMEM)] * 4,
        out_specs=pl.BlockSpec(memory_space=VMEM),
        compiler_params=pltpu.CompilerParams(vmem_limit_bytes=4 * 2**20),
        name="join_columns",
    )(*pieces)


def scatter_sum(v, me, move):
    v = v.reshape(v.shape[0], NX, v.shape[1] // NX, v.shape[2])

    def slot(k):
        return lax.dynamic_index_in_dim(v, (me + k) % NX, 1, keepdims=False)

    got = [move(slot(k), k) for k in (1, 3, 2)]
    return slot(0) + got[0] + got[1] + got[2]


def exchange_sum(v, move):
    got = [move(v, k) for k in (1, 3, 2)]
    return v + got[0] + got[1] + got[2]


def gather(v, move):
    got = {k: move(v, k) for k in (1, 3, 2)}
    return [v, got[1], got[2], got[3]]


def local(slab, start_basis, time_rank):
    rest_count = lax.axis_size("rest")
    columns_local = slab.shape[1]
    columns_all = columns_local * rest_count
    width = columns_local // NY
    ranks = start_basis.shape[1]
    _, _, first_me, _ = position()

    def scatter(send, keep):
        return scatter_sum(keep + along_core(send), first_me, lambda w, k: along_xz(w, k, True))

    def exchange(u):
        return exchange_sum(u, lambda w, k: along_xz(w, k, False))

    next_cols, last_cols = slices(slab)
    w1, w3 = along_y(next_cols, 1), along_y(last_cols, 3)
    send0, keep0, hl0, across = gram_call(own_kernel, "own_gram", [slab], [], 0, columns_local, 1, width)
    w1, w3, across = lax.optimization_barrier((w1, w3, across))
    w2 = along_y(across, 2)
    send, keep, hls = gram_call(early_kernel, "early_gram", [w1, w3, send0, keep0], [hl0], 4, width, 1, width)
    early = scatter(send, keep)
    early, w2 = lax.optimization_barrier((early, w2))
    early = exchange(early)
    send, keep = gram_call(late_kernel, "late_gram", [w2], [hls], 3, width, 0, width)
    late = exchange(scatter(send, keep))
    v = jnp.concatenate([early, late])
    got = {k: along_y(v, k) for k in (1, 3, 2)}
    at = [v, got[3], got[2], got[1]]

    def term(d, n):
        return at[d % NY][n]

    v = jnp.stack(
        [term(d, 1) + term(d + 1, 2) + term(d + 2, 5) + term(d + 3, 6) for d in range(NY)]
        + [term(d, 4) + term(d + 2, 4) + term(d + 1, 3) + term(d + 3, 3) for d in range(2)]
        + [term(d, 0) for d in range(NY)]
    )
    pieces = gather(v, lambda u, k: along_xz(u, k, True))
    pieces = pieces + [along_core(piece) for piece in pieces]
    basis, *cores, param = solve(time_rank, pieces, start_basis, hls, w2, 1.0 / columns_all)

    param = param + along_core(param)
    param = exchange_sum(param, lambda u, k: along_xz(u, k, True))
    param = exchange_sum(param, lambda u, k: along_xz(u, k, False))
    space_all = columns_local // PARAMS * rest_count
    param_gram = unpack_sum([param] + [along_y(param, k) for k in (1, 3, 2)], 1.0 / float(ranks * space_all))

    mine = {k: along_y(cores[k], k) for k in (1, 3, 2)}
    core = join_columns([cores[0], mine[1], mine[2], mine[3]])
    return (basis, core, param_gram)


def solution(mesh):
    in_specs = (P("tm", "rest"), P(), P())
    out_specs = (P(), P("tm", "rest"), P())
    return jax.shard_map(local, mesh=mesh, in_specs=in_specs, out_specs=out_specs, check_vma=False)
```
